512 devices in a mesh: gx: 32 (over x, y, core), gy: 16 (over z).
Axes of the slice: x: 4, y: 4, z: 16, core: 2. Of those that a mesh axis runs over, the one named last changes fastest.
Arguments:
- basis_vec: float32 [16, 512, 4096], P(None, 'gx', 'gy'), may hold values from -6 to 6
- conductivity: float32 [16, 512, 4096], P(None, 'gx', 'gy'), may hold values from 0.2 to 5
- sign_vals: int32 [512, 4096], P('gx', 'gy'), may hold values from -1 to 1, as said below
- sample_cols: int32 [256], P('gy'), may hold values from 0 to 255, as said below
Outputs:
- precond: float32 [16, 512, 4096], P(None, 'gx', 'gy')
- image_vec: float32 [16, 512, 4096], P(None, 'gx', 'gy')
- sketch: float32 [16, 512, 16], P(None, 'gx')
The draws below stay inside these ranges and needn't reach their ends.
Inputs may be any that keep to these rules, and one draw needn't show every extreme that they name: `sign_vals`: each entry is -1 or 1. `sample_cols`: the entries of each aligned block of 16 are distinct column offsets within one block of 256 columns.
All inputs are finite; a program needn't handle non-finite values.
Results may differ from the reference program's by a relative error of at most 0.0002.
Values sent between devices are 32-bit elements; how exact they have to be, the bound alone decides.
A program may use at most 64 MiB of HBM per device.

```python
import math
import jax
import jax.numpy as jnp
from jax import lax

DEPTH = 16
CX = 16
CY = 256
SWEEPS = 8
SAMPLES = 16
NX = 512
NY = 4096
N_GX = 32
N_GY = 16


def draw_sign_vals(key, part):
    return (2 * jax.random.randint(key, (NX, NY), 0, 2) - 1).astype(jnp.int32)


def draw_sample_cols(key, part):
    block_keys = jax.random.split(jax.random.fold_in(key, 7), NY // CY)

    def one_block(block_key):
        key_pick, key_mix = jax.random.split(block_key)
        middle_cols = jax.random.permutation(key_pick, CY - 2)[:SAMPLES - 2] + 1
        chosen = jnp.concatenate([jnp.array([0, CY - 1], jnp.int32), middle_cols.astype(jnp.int32)])
        return jax.random.permutation(key_mix, chosen)
    return jax.vmap(one_block)(block_keys).reshape(-1).astype(jnp.int32)


def levels(own_key, shape, cuts, least, top_value):
    level, own = 1.0, jax.random.fold_in(own_key, 6)
    for axis_at, blocks in cuts:
        steps = jnp.exp(jax.random.uniform(jax.random.fold_in(own, axis_at), (blocks,), jnp.float32, least / len(cuts), top_value / len(cuts)))
        level = level * jnp.repeat(steps, shape[axis_at] // blocks).reshape([-1 if axis == axis_at else 1 for axis in range(len(shape))])
    return level


def bell_draw(own_key, dims, width, reach, shards=(), kind=jnp.bfloat16):
    drawn = width * jax.random.normal(own_key, dims, jnp.float32)
    if shards:
        drawn = drawn * levels(own_key, dims, shards, -0.22, 0.18)
    return jnp.clip(drawn, -reach, reach).astype(kind)


def setup_inputs(seed: int = 0) -> dict:
    splits = jax.random.split(jax.random.key(seed), 5)
    return {
        "basis_vec": bell_draw(splits[0], (DEPTH, NX, NY), 1.0, 6.0, ((1, 32), (2, 16)), jnp.float32),
        "conductivity": jnp.clip(jnp.exp(math.log(5.0) - 3.218876 * jax.random.uniform(splits[1], (DEPTH, NX, NY), jnp.float32) ** levels(splits[1], (DEPTH, NX, NY), ((1, 32), (2, 16)), -0.2, 0.2)), 0.2, 5.0),
        "sign_vals": draw_sign_vals(jax.random.fold_in(splits[4], 71), 0),
        "sample_cols": draw_sample_cols(jax.random.fold_in(splits[4], 71), 0),
    }


reaction = 0.5
lowest = 0.5
highest = 62.0

def operate(values, conduct):
    padded = jnp.pad(values, ((1, 1), (0, 0), (0, 0)))
    centre_val = padded[1:-1, 1:-1, 1:-1]
    kappa_mid = conduct[1:-1, 1:-1, 1:-1]
    neighbours = ((padded[2:, 1:-1, 1:-1], conduct[2:, 1:-1, 1:-1]), (padded[:-2, 1:-1, 1:-1], conduct[:-2, 1:-1, 1:-1]), (padded[1:-1, 2:, 1:-1], conduct[1:-1, 2:, 1:-1]), (padded[1:-1, :-2, 1:-1], conduct[1:-1, :-2, 1:-1]), (padded[1:-1, 1:-1, 2:], conduct[1:-1, 1:-1, 2:]), (padded[1:-1, 1:-1, :-2], conduct[1:-1, 1:-1, :-2]))
    summed = reaction * centre_val
    for near_value, near_kappa in neighbours:
        summed = summed + 0.5 * (kappa_mid + near_kappa) * (centre_val - near_value)
    return summed

def hartley_table(length):
    row_ids = jnp.arange(length, dtype=jnp.int32)[:, None]
    col_ids = jnp.arange(length, dtype=jnp.int32)[None, :]
    angles = (row_ids * col_ids % length).astype(jnp.float32) * (2.0 * jnp.pi / length)
    return (jnp.cos(angles) + jnp.sin(angles)) / jnp.sqrt(jnp.float32(length))

def walsh_table(length):
    row_ids = jnp.arange(length, dtype=jnp.int32)[:, None]
    col_ids = jnp.arange(length, dtype=jnp.int32)[None, :]
    parity = jnp.zeros((length, length), jnp.int32)
    for shift_no in range(length.bit_length() - 1):
        parity = parity + (row_ids >> shift_no & 1) * (col_ids >> shift_no & 1)
    return (1 - 2 * (parity % 2)).astype(jnp.float32) / jnp.sqrt(jnp.float32(length))

def reference(basis_vec, conductivity, sign_vals, sample_cols):
    conduct = jnp.pad(conductivity, 1)

    def apply_grid(values):
        return operate(jnp.pad(values, ((0, 0), (1, 1), (1, 1))), conduct)
    middle = (highest + lowest) / 2.0
    spread = (highest - lowest) / 2.0
    sig_ratio = middle / spread
    rho_now = 1.0 / sig_ratio
    residual = basis_vec
    direction = residual * (1.0 / middle)
    precond = jnp.zeros_like(basis_vec)
    for sweep_no in range(SWEEPS):
        precond = precond + direction
        if sweep_no < SWEEPS - 1:
            residual = residual - apply_grid(direction)
            rho_next = 1.0 / (2.0 * sig_ratio - rho_now)
            direction = rho_next * rho_now * direction + 2.0 * rho_next / spread * residual
            rho_now = rho_next
    image_vec = apply_grid(precond)
    flipped = image_vec * sign_vals.astype(jnp.float32)[None]
    blocks = flipped.reshape(DEPTH, N_GX, CX, NY)
    mixed_vec = jnp.einsum('jk,dgkc->dgjc', hartley_table(CX), blocks, precision=lax.Precision.HIGHEST)
    mixed_vec = jnp.einsum('hg,dgjc->dhjc', walsh_table(N_GX), mixed_vec, precision=lax.Precision.HIGHEST)
    mixed_vec = mixed_vec.reshape(DEPTH, NX, NY)
    global_cols = sample_cols.reshape(N_GY, SAMPLES) + (jnp.arange(N_GY, dtype=jnp.int32) * CY)[:, None]
    picked = jnp.take(mixed_vec, global_cols.reshape(-1).astype(jnp.int32), axis=2)
    sketch = lax.optimization_barrier(jnp.sum(picked.reshape(DEPTH, NX, N_GY, SAMPLES), axis=2))
    return (precond, image_vec, sketch)
```

```python
import functools

import jax
import jax.numpy as jnp
import numpy as np
from jax import lax
from jax.experimental import pallas as pl
from jax.experimental.pallas import tpu as pltpu
from jax.sharding import PartitionSpec as P

SWEEPS = 8
HALO = SWEEPS
REACTION = 0.5
LOWEST = 0.5
HIGHEST = 62.0
MESH = pl.DeviceIdType.MESH
F32 = jnp.float32
BF16 = jnp.bfloat16


def split_bf16(x):
    high = x.astype(BF16)
    return high, (x - high.astype(F32)).astype(BF16)


def dot_nt(a, b):
    return lax.dot_general(a, b, (((1,), (1,)), ((), ())), preferred_element_type=F32)


def kernel(
    n_gx, n_gy,
    basis_hbm, kappa_hbm, sign_hbm, cols_hbm, mix_hbm,
    prec_hbm, image_hbm, sketch_hbm,
    in_u, in_k, in_sign, in_cols, in_mix,
    halo_u, halo_k, pack, strips,
    kap, fx, fy, fz, diag, res, dirn, prec, img, flip,
    out_p, out_i, pick, recv_1, part, recv_2, recv_3, out_s,
    load_sem, store_sem, row_send, row_recv, strip_send, strip_recv, step_send, step_recv,
):
    depth, rows, cols = in_u.shape
    wide = cols + 128
    lo, hi = HALO, HALO + rows
    total = rows + 2 * HALO
    samples = out_s.shape[2]
    share = samples // n_gy
    gx, gy = lax.axis_index("gx"), lax.axis_index("gy")
    has_up, has_down = gx > 0, gx < n_gx - 1
    has_left, has_right = gy > 0, gy < n_gy - 1

    loads = [
        pltpu.make_async_copy(src, dst, load_sem.at[i])
        for i, (src, dst) in enumerate(
            ((basis_hbm, in_u), (kappa_hbm, in_k), (sign_hbm, in_sign), (cols_hbm, in_cols), (mix_hbm, in_mix))
        )
    ]
    for load in loads:
        load.start()

    barrier = pltpu.get_barrier_semaphore()

    def greet(x, y):
        pl.semaphore_signal(barrier, inc=1, device_id=(x, y), device_id_type=MESH)

    def greet_col(t, c):
        greet(gx, lax.rem(gy + t, n_gy))
        return c

    def greet_row(t, c):
        greet(lax.rem(gx + t, n_gx), gy)
        return c

    lax.fori_loop(1, n_gy, greet_col, 0)
    lax.fori_loop(1, n_gx, greet_row, 0)
    vertical = ((-1, has_up), (1, has_down))
    sideways = ((-1, has_left), (1, has_right))
    for dx, ok_x in vertical:
        for dy, ok_y in sideways:
            @pl.when(ok_x & ok_y)
            def _():
                greet(gx + dx, gy + dy)
    n_diag = (has_up.astype(jnp.int32) + has_down.astype(jnp.int32)) * (
        has_left.astype(jnp.int32) + has_right.astype(jnp.int32)
    )

    def row_copy(array, k):
        source, target = ((in_u, halo_u), (in_k, halo_k))[array]
        first = rows - HALO if k == 0 else 0
        return pltpu.make_async_remote_copy(
            src_ref=source.at[:, pl.ds(first, HALO), :],
            dst_ref=target.at[k],
            send_sem=row_send.at[array, k],
            recv_sem=row_recv.at[array, k],
            device_id=(gx + (1 if k == 0 else -1), gy),
            device_id_type=MESH,
        )

    def strip_copy(side, dx):
        return pltpu.make_async_remote_copy(
            src_ref=pack.at[side],
            dst_ref=strips.at[side, 1 - dx],
            send_sem=strip_send.at[side, 1 - dx],
            recv_sem=strip_recv.at[side, 1 - dx],
            device_id=(gx + dx, gy + (1 if side == 0 else -1)),
            device_id_type=MESH,
        )

    loads[0].wait()
    loads[1].wait()
    pl.semaphore_wait(barrier, n_gx + n_gy - 2 + n_diag)
    send_ok = (has_down, has_up)
    recv_ok = (has_up, has_down)
    for k in range(2):
        @pl.when(send_ok[k])
        def _():
            row_copy(1, k).start()
            row_copy(0, k).start()

    lane = lax.broadcasted_iota(jnp.int32, (depth, 128), 1)
    for half in range(rows // 8):
        for source, target in ((in_u, res), (in_k, kap)):
            block = source[:, 8 * half:8 * half + 8, :]
            target[lo + 8 * half:lo + 8 * half + 8, :, 0:cols] = jnp.swapaxes(block, 0, 1)
    for array, source in enumerate((res, kap)):
        left = jnp.zeros((depth, 128), F32)
        right = jnp.zeros((depth, 128), F32)
        for i in range(rows):
            here = (lane >= 8 * i) & (lane < 8 * i + 8)
            right = jnp.where(here, pltpu.roll(source[lo + i, :, cols - 128:cols], (8 * i + 8) % 128, 1), right)
            first = source[lo + i, :, 0:128]
            left = jnp.where(here, pltpu.roll(first, 8 * i, 1) if i else first, left)
        pack[0, array] = right
        pack[1, array] = left

    side_ok = (has_right, has_left)
    for side in range(2):
        for dx in (0, -1, 1):
            ok = side_ok[side]
            if dx:
                ok = ok & (has_up if dx < 0 else has_down)

            @pl.when(ok)
            def _():
                strip_copy(side, dx).start()

    for k in range(2):
        @pl.when(jnp.logical_not(recv_ok[k]))
        def _():
            halo_u[k] = jnp.zeros(halo_u.shape[1:], F32)
            halo_k[k] = jnp.zeros(halo_k.shape[1:], F32)
    from_ok = (has_left, has_right)
    arrives = {}
    for side in range(2):
        for dx in (0, -1, 1):
            ok = from_ok[side]
            if dx:
                ok = ok & (has_up if dx > 0 else has_down)
            arrives[side, dx] = ok

            @pl.when(jnp.logical_not(ok))
            def _():
                strips[side, 1 - dx] = jnp.zeros(strips.shape[2:], F32)

    loads[3].wait()
    s_of = lax.broadcasted_iota(jnp.int32, (samples, cols), 0)
    c_of = lax.broadcasted_iota(jnp.int32, (samples, cols), 1)
    wanted = jnp.zeros((samples, cols), jnp.int32)
    for s in range(samples):
        wanted = jnp.where(s_of == s, in_cols[s], wanted)
    select = jnp.where(wanted == c_of, 1.0, 0.0).astype(BF16)

    for side in range(2):
        for dx in (0, -1, 1):
            @pl.when(arrives[side, dx])
            def _():
                strip_copy(side, dx).wait_recv()

    def ring(array, slot, packed_row):
        before = pltpu.roll(strips[0, slot, array], (120 - 8 * packed_row) % 128, 1)
        after = strips[1, slot, array]
        if packed_row:
            after = pltpu.roll(after, (128 - 8 * packed_row) % 128, 1)
        return jnp.where(lane < 8, after, jnp.where(lane >= 120, before, 0.0))

    for i in range(total):
        slot, packed_row = (0, rows - HALO + i) if i < lo else (1, i - lo) if i < hi else (2, i - hi)
        res[i, :, cols:wide] = ring(0, slot, packed_row)
        kap[i, :, cols:wide] = ring(1, slot, packed_row)

    for k in range(2):
        @pl.when(recv_ok[k])
        def _():
            row_copy(1, k).wait_recv()
            row_copy(0, k).wait_recv()
        first = 0 if k == 0 else hi
        for source, target in ((halo_u, res), (halo_k, kap)):
            target[first:first + HALO, :, 0:cols] = jnp.swapaxes(source[k], 0, 1)

    middle = (HIGHEST + LOWEST) / 2.0
    spread = (HIGHEST - LOWEST) / 2.0
    ratio = middle / spread
    d_of = lax.broadcasted_iota(jnp.int32, (depth, wide), 0)
    l_of = lax.broadcasted_iota(jnp.int32, (depth, wide), 1)
    at_left, at_right = gy == 0, gy == n_gy - 1
    outer_left = (l_of == 0) & at_left
    outer_right = (l_of == cols) & at_right
    half_y = jnp.where(outer_left | outer_right, 0.0, 0.5)
    half_z = jnp.where(d_of == 0, 0.0, 0.5)
    outer = (
        jnp.where((d_of == 0) | (d_of == depth - 1), 0.5, 0.0)
        + jnp.where(outer_left | ((l_of == cols - 1) & at_right), 0.5, 0.0)
    )

    def coefficients(i, before):
        here = kap[i]
        shut = ((i == lo) & (gx == 0)) | ((i == hi) & (gx == n_gx - 1))
        edge = ((i == lo) & (gx == 0)) | ((i == hi - 1) & (gx == n_gx - 1))
        fx[i] = jnp.where(shut, 0.0, 0.5) * (here + before)
        fy[i] = half_y * (here + pltpu.roll(here, 1, 1))
        fz[i] = half_z * (here + pltpu.roll(here, 1, 0))
        diag[i] = REACTION + (outer + jnp.where(edge, 0.5, 0.0)) * here
        dirn[i] = res[i] * (1.0 / middle)
        return here

    dirn[0] = res[0] * (1.0 / middle)
    lax.fori_loop(1, total, coefficients, kap[0])

    def applied(u, u_next, flux, face, i):
        flux_next = face * (u_next - u)
        flux_y = fy[i] * (u - pltpu.roll(u, 1, 1))
        flux_z = fz[i] * (u - pltpu.roll(u, 1, 0))
        out = diag[i] * u + (flux - flux_next)
        out = out + (flux_y - pltpu.roll(flux_y, wide - 1, 1))
        out = out + (flux_z - pltpu.roll(flux_z, depth - 1, 0))
        return out, flux_next

    rho = 1.0 / ratio
    for sweep in range(SWEEPS - 1):
        reach = HALO - 1 - sweep
        rho_next = 1.0 / (2.0 * ratio - rho)
        keep, gain = rho_next * rho, 2.0 * rho_next / spread
        rho = rho_next

        def row(i, carry, sweep=sweep, keep=keep, gain=gain):
            u, flux = carry
            u_next = dirn[i + 1]
            au, flux = applied(u, u_next, flux, fx[i + 1], i)
            left_over = res[i] - au
            res[i] = left_over
            new = keep * u + gain * left_over
            dirn[i] = new
            prec[i] = (u if sweep == 0 else prec[i]) + new
            return u_next, flux

        start = lo - reach
        u0 = dirn[start]
        lax.fori_loop(start, hi + reach, row, (u0, fx[start] * (u0 - dirn[start - 1])))

    for half in range(rows // 8):
        block = prec[lo + 8 * half:lo + 8 * half + 8, :, 0:cols]
        out_p[:, 8 * half:8 * half + 8, :] = jnp.swapaxes(block, 0, 1)
    store_p = pltpu.make_async_copy(out_p, prec_hbm, store_sem.at[0])
    store_p.start()

    loads[2].wait()

    def last(i, carry):
        u, flux = carry
        u_next = prec[i + 1]
        au, flux = applied(u, u_next, flux, fx[i + 1], i)
        own = au[:, 0:cols]
        img[i - lo] = own
        flip[i - lo] = own * in_sign[pl.ds(i - lo, 1), :].astype(F32)
        return u_next, flux

    u0 = prec[lo]
    lax.fori_loop(lo, hi, last, (u0, fx[lo] * (u0 - prec[lo - 1])))

    high, low = split_bf16(flip[...].reshape(rows * depth, cols))
    pick[...] = dot_nt(select, high) + dot_nt(select, low)

    def exchange(step, source, target, device):
        return pltpu.make_async_remote_copy(
            src_ref=source, dst_ref=target, send_sem=step_send.at[step], recv_sem=step_recv.at[step],
            device_id=device, device_id_type=MESH,
        )

    mine = pl.ds(gy * share, share)

    def scatter(t, c):
        peer = lax.rem(gy + t, n_gy)
        exchange(0, pick.at[pl.ds(peer * share, share)], recv_1.at[gy], (gx, peer)).start()
        return c

    lax.fori_loop(1, n_gy, scatter, 0)
    recv_1[gy] = pick[mine, :]

    for half in range(rows // 8):
        out_i[:, 8 * half:8 * half + 8, :] = jnp.swapaxes(img[8 * half:8 * half + 8], 0, 1)
    store_i = pltpu.make_async_copy(out_i, image_hbm, store_sem.at[1])
    store_i.start()

    others_x, others_y = recv_2.at[pl.ds(0, n_gx - 1)], recv_1.at[pl.ds(0, n_gy - 1)]
    wait_1 = exchange(0, others_y, others_y, (gx, gy))
    wait_1.wait_recv()

    part[...] = jnp.sum(recv_1[...], axis=0)

    def gather_x(t, c):
        peer = lax.rem(gx + t, n_gx)
        exchange(1, part, recv_2.at[gx], (peer, gy)).start()
        return c

    lax.fori_loop(1, n_gx, gather_x, 0)
    recv_2[gx] = part[...]
    both = (lax.broadcasted_iota(jnp.int32, (n_gx, share, rows * depth), 0)) & gx
    parity = jnp.zeros_like(both)
    for bit in range(n_gx.bit_length() - 1):
        parity = parity ^ (both >> bit & 1)
    walsh = (1 - 2 * parity).astype(F32) * (1.0 / n_gx ** 0.5)
    wait_2 = exchange(1, others_x, others_x, (gx, gy))
    wait_2.wait_recv()
    recv_3[mine, :] = jnp.sum(recv_2[...] * walsh, axis=0)

    def gather_y(t, c):
        peer = lax.rem(gy + t, n_gy)
        exchange(2, recv_3.at[mine], recv_3.at[mine], (gx, peer)).start()
        return c

    lax.fori_loop(1, n_gy, gather_y, 0)
    loads[4].wait()
    wait_3 = exchange(2, others_y, others_y, (gx, gy))
    wait_3.wait_recv()
    high, low = split_bf16(recv_3[...])
    mixed = dot_nt(in_mix[0], high) + dot_nt(in_mix[0], low) + dot_nt(in_mix[1], high)
    out_s[...] = mixed.reshape(out_s.shape)
    store_s = pltpu.make_async_copy(out_s, sketch_hbm, store_sem.at[2])
    store_s.start()

    for k in range(2):
        @pl.when(send_ok[k])
        def _():
            row_copy(1, k).wait_send()
            row_copy(0, k).wait_send()
    for side in range(2):
        for dx in (0, -1, 1):
            ok = side_ok[side]
            if dx:
                ok = ok & (has_up if dx < 0 else has_down)

            @pl.when(ok)
            def _():
                strip_copy(side, dx).wait_send()
    wait_1.wait_send()
    wait_2.wait_send()
    wait_3.wait_send()
    store_p.wait()
    store_i.wait()
    store_s.wait()


def per_device(n_gx, n_gy, basis_vec, conductivity, sign_vals, sample_cols):
    depth, rows, cols = basis_vec.shape
    samples = sample_cols.shape[0]
    share = samples // n_gy
    wide, total = cols + 128, rows + 2 * HALO
    index = np.arange(rows)
    angle = (index[:, None] * index[None, :] % rows) * (2.0 * np.pi / rows)
    hartley = (np.cos(angle) + np.sin(angle)) / np.sqrt(rows)
    mix = np.einsum("jk,de->djke", hartley, np.eye(depth)).reshape(depth * rows, rows * depth).astype(np.float32)
    mix_high = mix.astype(jnp.bfloat16)
    mix_low = (mix - mix_high.astype(np.float32)).astype(jnp.bfloat16)
    mix = jnp.asarray(np.stack([mix_high, mix_low]))

    field = (depth, rows, cols)
    tall = pltpu.VMEM((total, depth, wide), F32)
    scratch = [
        pltpu.VMEM(field, F32), pltpu.VMEM(field, F32), pltpu.VMEM((rows, cols), jnp.int32),
        pltpu.SMEM((samples,), jnp.int32), pltpu.VMEM(mix.shape, BF16),
        pltpu.VMEM((2, depth, HALO, cols), F32), pltpu.VMEM((2, depth, HALO, cols), F32),
        pltpu.VMEM((2, 2, depth, 128), F32), pltpu.VMEM((2, 3, 2, depth, 128), F32),
        tall, tall, tall, tall, tall, tall, tall, tall,
        pltpu.VMEM((rows, depth, cols), F32), pltpu.VMEM((rows, depth, cols), F32),
        pltpu.VMEM(field, F32), pltpu.VMEM(field, F32),
        pltpu.VMEM((samples, rows * depth), F32), pltpu.VMEM((n_gy, share, rows * depth), F32),
        pltpu.VMEM((share, rows * depth), F32), pltpu.VMEM((n_gx, share, rows * depth), F32),
        pltpu.VMEM((samples, rows * depth), F32), pltpu.VMEM((depth, rows, samples), F32),
        pltpu.SemaphoreType.DMA((5,)), pltpu.SemaphoreType.DMA((3,)),
        pltpu.SemaphoreType.DMA((2, 2)), pltpu.SemaphoreType.DMA((2, 2)),
        pltpu.SemaphoreType.DMA((2, 3)), pltpu.SemaphoreType.DMA((2, 3)),
        pltpu.SemaphoreType.DMA((3,)), pltpu.SemaphoreType.DMA((3,)),
    ]
    return pl.pallas_call(
        functools.partial(kernel, n_gx, n_gy),
        out_shape=(
            jax.ShapeDtypeStruct(field, F32),
            jax.ShapeDtypeStruct(field, F32),
            jax.ShapeDtypeStruct((depth, rows, samples), F32),
        ),
        in_specs=[pl.BlockSpec(memory_space=pl.ANY)] * 5,
        out_specs=(pl.BlockSpec(memory_space=pl.ANY),) * 3,
        scratch_shapes=scratch,
        compiler_params=pltpu.CompilerParams(
            collective_id=0, has_side_effects=True, vmem_limit_bytes=32 * 1024 * 1024
        ),
    )(basis_vec, conductivity, sign_vals, sample_cols, mix)


def solution(mesh):
    in_specs = (P(None, "gx", "gy"), P(None, "gx", "gy"), P("gx", "gy"), P("gy"))
    out_specs = (P(None, "gx", "gy"), P(None, "gx", "gy"), P(None, "gx", None))
    return jax.shard_map(
        functools.partial(per_device, mesh.shape["gx"], mesh.shape["gy"]),
        mesh=mesh, in_specs=in_specs, out_specs=out_specs, check_vma=False,
    )
```

```python
import functools

import jax
import jax.numpy as jnp
import numpy as np
from jax import lax
from jax.experimental import pallas as pl
from jax.experimental.pallas import tpu as pltpu
from jax.sharding import PartitionSpec as P

SWEEPS = 8
HALO = SWEEPS
REACTION = 0.5
LOWEST = 0.5
HIGHEST = 62.0
MESH = pl.DeviceIdType.MESH
F32 = jnp.float32
BF16 = jnp.bfloat16
COEF_ROWS = 5
COPIES = 4
SWEEP_ROWS = {30: 10, 28: 14, 26: 13, 24: 12, 22: 11, 20: 10, 18: 9}


def far_first(count):
    return sorted(range(1, count), key=lambda t: -min(t, count - t))


def far_in_plane(count):
    def hops(t):
        y, x = t // 2 % 4, t // 8
        return min(y, 4 - y) + min(x, 4 - x)
    return sorted(range(1, count), key=lambda t: -hops(t))


def split_bf16(x):
    high = x.astype(BF16)
    return high, (x - high.astype(F32)).astype(BF16)


def looped(first, end, count, body):
    steps = (end - first) // count

    def step(t, c):
        body(first + t * count, count)
        return c

    lax.fori_loop(0, steps, step, 0)
    if (end - first) % count:
        body(first + steps * count, (end - first) % count)


def dot_nt(a, b):
    return lax.dot_general(a, b, (((1,), (1,)), ((), ())), preferred_element_type=F32)


def kernel(
    n_gx, n_gy,
    basis_hbm, kappa_hbm, sign_hbm, cols_hbm, mix_hbm,
    out_p, out_i, out_s,
    in_u, in_k, in_sign, in_cols, in_mix,
    halo_u, halo_k, pack, strips,
    kap, fx, fy, fy2, fz, diag, base, prec_a, prec_b, img, flip,
    pick, recv_1, part, recv_2, recv_3,
    load_sem, row_send, row_recv, strip_send, strip_recv, step_send, step_recv, token_x, token_y,
):
    depth, rows, cols = in_u.shape
    wide = cols + 128
    lo, hi = HALO, HALO + rows
    total = rows + 2 * HALO
    samples = out_s.shape[2]
    pieces, share = recv_3.shape[0], recv_3.shape[1]
    gx, gy = lax.axis_index("gx"), lax.axis_index("gy")
    has_up, has_down = gx > 0, gx < n_gx - 1
    has_left, has_right = gy > 0, gy < n_gy - 1

    loads = [
        pltpu.make_async_copy(src, dst, load_sem.at[i])
        for i, (src, dst) in enumerate(
            ((basis_hbm, in_u), (kappa_hbm, in_k), (sign_hbm, in_sign), (cols_hbm, in_cols), (mix_hbm, in_mix))
        )
    ]
    for load in loads:
        load.start()

    barrier = pltpu.get_barrier_semaphore()

    def around_x(t):
        return lax.rem(gx + t + n_gx, n_gx), gy

    def around_y(t):
        return gx, lax.rem(gy + t + n_gy, n_gy)

    def tell(semaphore, device):
        pl.semaphore_signal(semaphore, inc=1, device_id=device, device_id_type=MESH)

    for t in (1, -1):
        tell(barrier, around_y(t))
        tell(barrier, around_x(t))
    vertical = ((-1, has_up), (1, has_down))
    sideways = ((-1, has_left), (1, has_right))
    for dx, ok_x in vertical:
        for dy, ok_y in sideways:
            @pl.when(ok_x & ok_y)
            def _():
                tell(barrier, (gx + dx, gy + dy))
    n_diag = (has_up.astype(jnp.int32) + has_down.astype(jnp.int32)) * (
        has_left.astype(jnp.int32) + has_right.astype(jnp.int32)
    )

    def token(round_no, action):
        distance = 1 << round_no
        for count, around, semaphores in ((n_gy, around_y, token_y), (n_gx, around_x, token_x)):
            if distance < count // 2:
                if action == "tell":
                    tell(semaphores.at[round_no], around(distance))
                    tell(semaphores.at[round_no], around(-distance))
                else:
                    pl.semaphore_wait(semaphores.at[round_no], 2)

    def row_copy(array, k):
        source, target = ((in_u, halo_u), (in_k, halo_k))[array]
        first = rows - HALO if k == 0 else 0
        return pltpu.make_async_remote_copy(
            src_ref=source.at[:, pl.ds(first, HALO), :],
            dst_ref=target.at[k],
            send_sem=row_send.at[array, k],
            recv_sem=row_recv.at[array, k],
            device_id=(gx + (1 if k == 0 else -1), gy),
            device_id_type=MESH,
        )

    def strip_copy(side, dx):
        return pltpu.make_async_remote_copy(
            src_ref=pack.at[side],
            dst_ref=strips.at[side, 1 - dx],
            send_sem=strip_send.at[side, 1 - dx],
            recv_sem=strip_recv.at[side, 1 - dx],
            device_id=(gx + dx, gy + (1 if side == 0 else -1)),
            device_id_type=MESH,
        )

    loads[0].wait()
    loads[1].wait()
    pl.semaphore_wait(barrier, 4 + n_diag)
    token(0, "tell")
    send_ok = (has_down, has_up)
    recv_ok = (has_up, has_down)
    for k in range(2):
        @pl.when(send_ok[k])
        def _():
            row_copy(1, k).start()
            row_copy(0, k).start()

    half_d = depth // 2

    def place(block, target, first):
        block = block.reshape(half_d, 2, 8, cols)
        for odd in range(2):
            target[first:first + 8, odd * half_d:(odd + 1) * half_d, 0:cols] = jnp.swapaxes(block[:, odd], 0, 1)

    def put_back(source, first, target, row0):
        for odd in range(2):
            block = jnp.swapaxes(source[first:first + 8, odd * half_d:(odd + 1) * half_d, 0:cols], 0, 1)
            for m in range(half_d):
                target[2 * m + odd, row0:row0 + 8, :] = block[m]

    lane = lax.broadcasted_iota(jnp.int32, (depth, 128), 1)
    for part_no in range(rows // 8):
        for source, target in ((in_u, base), (in_k, kap)):
            place(source[:, 8 * part_no:8 * part_no + 8, :], target, lo + 8 * part_no)
    for array, source in enumerate((base, kap)):
        left = jnp.zeros((depth, 128), F32)
        right = jnp.zeros((depth, 128), F32)
        for i in range(rows):
            here = (lane >= 8 * i) & (lane < 8 * i + 8)
            right = jnp.where(here, pltpu.roll(source[lo + i, :, cols - 128:cols], (8 * i + 8) % 128, 1), right)
            first = source[lo + i, :, 0:128]
            left = jnp.where(here, pltpu.roll(first, 8 * i, 1) if i else first, left)
        pack[0, array] = right
        pack[1, array] = left

    side_ok = (has_right, has_left)
    for side in range(2):
        for dx in (0, -1, 1):
            ok = side_ok[side]
            if dx:
                ok = ok & (has_up if dx < 0 else has_down)

            @pl.when(ok)
            def _():
                strip_copy(side, dx).start()

    for k in range(2):
        @pl.when(jnp.logical_not(recv_ok[k]))
        def _():
            halo_u[k] = jnp.zeros(halo_u.shape[1:], F32)
            halo_k[k] = jnp.zeros(halo_k.shape[1:], F32)
    from_ok = (has_left, has_right)
    arrives = {}
    for side in range(2):
        for dx in (0, -1, 1):
            ok = from_ok[side]
            if dx:
                ok = ok & (has_up if dx > 0 else has_down)
            arrives[side, dx] = ok

            @pl.when(jnp.logical_not(ok))
            def _():
                strips[side, 1 - dx] = jnp.zeros(strips.shape[2:], F32)

    loads[3].wait()
    s_of = lax.broadcasted_iota(jnp.int32, (samples, cols), 0)
    c_of = lax.broadcasted_iota(jnp.int32, (samples, cols), 1)
    wanted = jnp.zeros((samples, cols), jnp.int32)
    for s in range(samples):
        wanted = jnp.where(s_of == s, in_cols[s], wanted)
    select = jnp.where(wanted == c_of, 1.0, 0.0).astype(BF16)

    for side in range(2):
        for dx in (0, -1, 1):
            @pl.when(arrives[side, dx])
            def _():
                strip_copy(side, dx).wait_recv()

    token(0, "wait")
    token(1, "tell")

    def ring(array, slot, packed_row):
        before = pltpu.roll(strips[0, slot, array], (120 - 8 * packed_row) % 128, 1)
        after = strips[1, slot, array]
        if packed_row:
            after = pltpu.roll(after, (128 - 8 * packed_row) % 128, 1)
        return jnp.where(lane < 8, after, jnp.where(lane >= 120, before, 0.0))

    for i in range(total):
        slot, packed_row = (0, rows - HALO + i) if i < lo else (1, i - lo) if i < hi else (2, i - hi)
        base[i, :, cols:wide] = ring(0, slot, packed_row)
        kap[i, :, cols:wide] = ring(1, slot, packed_row)

    for k in range(2):
        @pl.when(recv_ok[k])
        def _():
            row_copy(1, k).wait_recv()
            row_copy(0, k).wait_recv()
        first = 0 if k == 0 else hi
        for source, target in ((halo_u, base), (halo_k, kap)):
            place(source[k], target, first)

    token(1, "wait")
    token(2, "tell")

    middle = (HIGHEST + LOWEST) / 2.0
    spread = (HIGHEST - LOWEST) / 2.0
    ratio = middle / spread
    p_of = lax.broadcasted_iota(jnp.int32, (depth, wide), 0)
    l_of = lax.broadcasted_iota(jnp.int32, (depth, wide), 1)
    at_left, at_right = gy == 0, gy == n_gy - 1
    face_0, face_1 = (l_of == 0) & at_left, (l_of == cols) & at_right
    half_y = jnp.where(face_0 | face_1, 0.0, 0.5)
    half_y2 = jnp.where(((l_of == wide - 1) & at_left) | ((l_of == cols - 1) & at_right), 0.0, 0.5)
    half_z = jnp.where(p_of[0:half_d] == half_d - 1, 0.0, 0.5)
    outer = (
        jnp.where((p_of == 0) | (p_of == depth - 1), 0.5, 0.0)
        + jnp.where(face_0 | ((l_of == cols - 1) & at_right), 0.5, 0.0)
    )

    def coefficients(first, count):
        before = kap[first - 1]
        for j in range(count):
            i = first + j
            here = kap[i]
            even, odd = here[0:half_d], here[half_d:depth]
            fx[i] = 0.5 * (here + before)
            fy[i] = half_y * (here + pltpu.roll(here, 1, 1))
            fy2[i] = half_y2 * (here + pltpu.roll(here, wide - 1, 1))
            fz[i, 0:half_d] = 0.5 * (even + odd)
            fz[i, half_d:depth] = half_z * (odd + pltpu.roll(even, half_d - 1, 0))
            diag[i] = REACTION + outer * here
            prec_a[i] = base[i] * (1.0 / middle)
            before = here

    looped(1, total - 1, COEF_ROWS, coefficients)
    fx[total - 1] = 0.5 * (kap[total - 1] + kap[total - 2])
    for i in (0, total - 1):
        prec_a[i] = base[i] * (1.0 / middle)
    for inner, face, ok in ((lo, lo, has_up), (hi - 1, hi, has_down)):
        @pl.when(jnp.logical_not(ok))
        def _():
            fx[face] = jnp.zeros((depth, wide), F32)
            diag[inner] = diag[inner] + 0.5 * kap[inner]

    def applied(source, i, count):
        u = [source[i + j] for j in range(-1, count + 1)]
        flux = [fx[i + j] * (u[j + 1] - u[j]) for j in range(count + 1)]
        for j in range(count):
            here = u[j + 1]
            left = fy[i + j] * (here - pltpu.roll(here, 1, 1))
            right = fy2[i + j] * (pltpu.roll(here, wide - 1, 1) - here)
            out = diag[i + j] * here + (flux[j] - flux[j + 1])
            out = out + (left - right)
            even, odd = here[0:half_d], here[half_d:depth]
            inside = fz[i + j, 0:half_d] * (odd - even)
            between = fz[i + j, half_d:depth] * (pltpu.roll(even, half_d - 1, 0) - odd)
            out_even = out[0:half_d] + (pltpu.roll(between, 1, 0) - inside)
            out_odd = out[half_d:depth] + (inside - between)
            yield j, here, jnp.concatenate([out_even, out_odd], axis=0)

    rho = 1.0 / ratio
    buffers = (prec_a, prec_b)
    for sweep in range(SWEEPS - 1):
        reach = HALO - 1 - sweep
        rho_next = 1.0 / (2.0 * ratio - rho)
        keep, gain = rho_next * rho, 2.0 * rho_next / spread
        rho = rho_next
        source, target = buffers[sweep % 2], buffers[(sweep + 1) % 2]

        def advance(i, count, sweep=sweep, keep=keep, gain=gain, source=source, target=target):
            for j, here, au in applied(source, i, count):
                change = here if sweep == 0 else here - target[i + j]
                target[i + j] = (here + keep * change) + gain * (base[i + j] - au)

        looped(lo - reach, hi + reach, SWEEP_ROWS[rows + 2 * reach], advance)
        if sweep == 3:
            token(2, "wait")
            token(3, "tell")

    prec = buffers[(SWEEPS - 1) % 2]
    loads[2].wait()

    def last(i, count):
        for j, here, au in applied(prec, i, count):
            own = au[:, 0:cols]
            img[i - lo + j] = own
            flip[i - lo + j] = own * in_sign[pl.ds(i - lo + j, 1), :].astype(F32)

    looped(lo, hi, 8, last)

    high, low = split_bf16(flip[...].reshape(rows * depth, cols))
    picked = dot_nt(select, high) + dot_nt(select, low)
    for q in range(pieces):
        pick[q] = picked[q * share:(q + 1) * share]
    token(3, "wait")

    def exchange(step, source, target, device):
        return pltpu.make_async_remote_copy(
            src_ref=source, dst_ref=target, send_sem=step_send.at[step], recv_sem=step_recv.at[step],
            device_id=device, device_id_type=MESH,
        )

    for t in far_first(n_gy):
        peer = lax.rem(gy + t, n_gy)
        exchange(0, pick.at[lax.rem(peer, pieces)], recv_1.at[gy], (gx, peer)).start()
    mine = lax.rem(gy, pieces)
    recv_1[gy] = pick[mine]

    for part_no in range(rows // 8):
        put_back(img, 8 * part_no, out_i, 8 * part_no)
        put_back(prec, lo + 8 * part_no, out_p, 8 * part_no)

    others_x, others_y = recv_2.at[pl.ds(0, n_gx - 1)], recv_1.at[pl.ds(0, n_gy - 1)]
    wait_1 = exchange(0, others_y, others_y, (gx, gy))
    wait_1.wait_recv()
    part[...] = jnp.sum(recv_1[...], axis=0)

    for t in far_in_plane(n_gx):
        exchange(1, part, recv_2.at[gx], around_x(t)).start()
    recv_2[gx] = part[...]
    both = lax.broadcasted_iota(jnp.int32, (n_gx, share, rows * depth), 0) & gx
    parity = jnp.zeros_like(both)
    for bit in range(n_gx.bit_length() - 1):
        parity = parity ^ (both >> bit & 1)
    walsh = (1 - 2 * parity).astype(F32) * (1.0 / n_gx ** 0.5)
    wait_2 = exchange(1, others_x, others_x, (gx, gy))
    wait_2.wait_recv()
    recv_3[mine] = jnp.sum(recv_2[...] * walsh, axis=0)

    near = [t - pieces // 2 for t in range(pieces) if t != pieces // 2]
    for t in sorted(near, key=abs, reverse=True):
        exchange(2, recv_3.at[mine], recv_3.at[mine], around_y(t)).start()
    loads[4].wait()
    wait_3 = None
    if near:
        others_near = recv_1.at[pl.ds(0, pieces - 1)]
        wait_3 = exchange(2, others_near, others_near, (gx, gy))
        wait_3.wait_recv()
    high, low = split_bf16(jnp.concatenate([recv_3[q] for q in range(pieces)], axis=0))
    mixed = dot_nt(in_mix[0], high) + dot_nt(in_mix[0], low) + dot_nt(in_mix[1], high)
    out_s[...] = mixed.reshape(out_s.shape)

    for k in range(2):
        @pl.when(send_ok[k])
        def _():
            row_copy(1, k).wait_send()
            row_copy(0, k).wait_send()
    for side in range(2):
        for dx in (0, -1, 1):
            ok = side_ok[side]
            if dx:
                ok = ok & (has_up if dx < 0 else has_down)

            @pl.when(ok)
            def _():
                strip_copy(side, dx).wait_send()
    wait_1.wait_send()
    wait_2.wait_send()
    if wait_3 is not None:
        wait_3.wait_send()


def per_device(n_gx, n_gy, basis_vec, conductivity, sign_vals, sample_cols):
    depth, rows, cols = basis_vec.shape
    samples = sample_cols.shape[0]
    pieces = max(n_gy // COPIES, 1)
    share = samples // pieces
    wide, total = cols + 128, rows + 2 * HALO
    index = np.arange(rows)
    angle = (index[:, None] * index[None, :] % rows) * (2.0 * np.pi / rows)
    hartley = (np.cos(angle) + np.sin(angle)) / np.sqrt(rows)
    order = np.concatenate([np.arange(0, depth, 2), np.arange(1, depth, 2)])
    mix = np.einsum("jk,de->djke", hartley, np.eye(depth)[:, order]).reshape(depth * rows, rows * depth).astype(np.float32)
    mix_high = mix.astype(jnp.bfloat16)
    mix_low = (mix - mix_high.astype(np.float32)).astype(jnp.bfloat16)
    mix = jnp.asarray(np.stack([mix_high, mix_low]))

    field = (depth, rows, cols)
    tall = pltpu.VMEM((total, depth, wide), F32)
    scratch = [
        pltpu.VMEM(field, F32), pltpu.VMEM(field, F32), pltpu.VMEM((rows, cols), jnp.int32),
        pltpu.SMEM((samples,), jnp.int32), pltpu.VMEM(mix.shape, BF16),
        pltpu.VMEM((2, depth, HALO, cols), F32), pltpu.VMEM((2, depth, HALO, cols), F32),
        pltpu.VMEM((2, 2, depth, 128), F32), pltpu.VMEM((2, 3, 2, depth, 128), F32),
        tall, tall, tall, tall, tall, tall, tall, tall, tall,
        pltpu.VMEM((rows, depth, cols), F32), pltpu.VMEM((rows, depth, cols), F32),
        pltpu.VMEM((pieces, share, rows * depth), F32), pltpu.VMEM((n_gy, share, rows * depth), F32),
        pltpu.VMEM((share, rows * depth), F32), pltpu.VMEM((n_gx, share, rows * depth), F32),
        pltpu.VMEM((pieces, share, rows * depth), F32),
        pltpu.SemaphoreType.DMA((5,)),
        pltpu.SemaphoreType.DMA((2, 2)), pltpu.SemaphoreType.DMA((2, 2)),
        pltpu.SemaphoreType.DMA((2, 3)), pltpu.SemaphoreType.DMA((2, 3)),
        pltpu.SemaphoreType.DMA((3,)), pltpu.SemaphoreType.DMA((3,)),
        pltpu.SemaphoreType.REGULAR((4,)), pltpu.SemaphoreType.REGULAR((4,)),
    ]
    return pl.pallas_call(
        functools.partial(kernel, n_gx, n_gy),
        out_shape=(
            jax.ShapeDtypeStruct(field, F32),
            jax.ShapeDtypeStruct(field, F32),
            jax.ShapeDtypeStruct((depth, rows, samples), F32),
        ),
        in_specs=[pl.BlockSpec(memory_space=pltpu.HBM)] * 5,
        out_specs=(pl.BlockSpec(memory_space=pltpu.VMEM),) * 3,
        scratch_shapes=scratch,
        compiler_params=pltpu.CompilerParams(
            collective_id=0, has_side_effects=True, vmem_limit_bytes=59000 * 1024
        ),
    )(basis_vec, conductivity, sign_vals, sample_cols, mix)


def solution(mesh):
    in_specs = (P(None, "gx", "gy"), P(None, "gx", "gy"), P("gx", "gy"), P("gy"))
    out_specs = (P(None, "gx", "gy"), P(None, "gx", "gy"), P(None, "gx", None))
    return jax.shard_map(
        functools.partial(per_device, mesh.shape["gx"], mesh.shape["gy"]),
        mesh=mesh, in_specs=in_specs, out_specs=out_specs, check_vma=False,
    )
```

```python
import functools

import jax
import jax.numpy as jnp
import numpy as np
from jax import lax
from jax.experimental import pallas as pl
from jax.experimental.pallas import tpu as pltpu
from jax.sharding import PartitionSpec as P

SWEEPS = 8
HALO = SWEEPS
REACTION = 0.5
LOWEST = 0.5
HIGHEST = 62.0
MESH = pl.DeviceIdType.MESH
F32 = jnp.float32
BF16 = jnp.bfloat16
COPIES = 4
LAST_KIB = 59000


def far_first(count):
    return sorted(range(1, count), key=lambda t: -min(t, count - t))


def far_in_plane(count):
    def hops(t):
        y, x = t // 2 % 4, t // 8
        return min(y, 4 - y) + min(x, 4 - x)
    return sorted(range(1, count), key=lambda t: -hops(t))


def split_bf16(x):
    high = x.astype(BF16)
    return high, (x - high.astype(F32)).astype(BF16)


def looped(first, end, count, body):
    steps = (end - first) // count

    def step(t, c):
        body(first + t * count, count)
        return c

    lax.fori_loop(0, steps, step, 0)
    if (end - first) % count:
        body(first + steps * count, (end - first) % count)


def dot_nt(a, b):
    return lax.dot_general(a, b, (((1,), (1,)), ((), ())), preferred_element_type=F32)


def kernel(
    n_gx, n_gy,
    basis_hbm, kappa_hbm, sign_hbm, cols_hbm, mix_hbm,
    prec_hbm, image_hbm, sketch_hbm,
    in_u, in_k, in_sign, in_cols, in_mix,
    halo_u, halo_k, pack, strips,
    kap, fx, fy, fy2, fz, diag, base, prec_a, prec_b, img, flip,
    pick, recv_1, part, recv_2, recv_3, out_p, out_i, out_s,
    load_sem, store_sem, row_send, row_recv, strip_send, strip_recv, step_send, step_recv, token_x, token_y,
):
    depth, rows, cols = in_u.shape
    wide = cols + 128
    lo, hi = HALO, HALO + rows
    total = rows + 2 * HALO
    samples = out_s.shape[2]
    pieces, share = recv_3.shape[0], recv_3.shape[1]
    gx, gy = lax.axis_index("gx"), lax.axis_index("gy")
    has_up, has_down = gx > 0, gx < n_gx - 1
    has_left, has_right = gy > 0, gy < n_gy - 1

    loads = [
        pltpu.make_async_copy(src, dst, load_sem.at[i])
        for i, (src, dst) in enumerate(
            ((basis_hbm, in_u), (kappa_hbm, in_k), (sign_hbm, in_sign), (cols_hbm, in_cols), (mix_hbm, in_mix))
        )
    ]
    for load in loads:
        load.start()

    barrier = pltpu.get_barrier_semaphore()

    def around_x(t):
        return lax.rem(gx + t + n_gx, n_gx), gy

    def around_y(t):
        return gx, lax.rem(gy + t + n_gy, n_gy)

    def tell(semaphore, device):
        pl.semaphore_signal(semaphore, inc=1, device_id=device, device_id_type=MESH)

    for t in (1, -1):
        tell(barrier, around_y(t))
        tell(barrier, around_x(t))
    vertical = ((-1, has_up), (1, has_down))
    sideways = ((-1, has_left), (1, has_right))
    for dx, ok_x in vertical:
        for dy, ok_y in sideways:
            @pl.when(ok_x & ok_y)
            def _():
                tell(barrier, (gx + dx, gy + dy))
    n_diag = (has_up.astype(jnp.int32) + has_down.astype(jnp.int32)) * (
        has_left.astype(jnp.int32) + has_right.astype(jnp.int32)
    )

    def token(round_no, action):
        distance = 1 << round_no
        for count, around, semaphores in ((n_gy, around_y, token_y), (n_gx, around_x, token_x)):
            if distance < count // 2:
                if action == "tell":
                    tell(semaphores.at[round_no], around(distance))
                    tell(semaphores.at[round_no], around(-distance))
                else:
                    pl.semaphore_wait(semaphores.at[round_no], 2)

    def row_copy(array, k):
        source, target = ((in_u, halo_u), (in_k, halo_k))[array]
        first = rows - HALO if k == 0 else 0
        return pltpu.make_async_remote_copy(
            src_ref=source.at[:, pl.ds(first, HALO), :],
            dst_ref=target.at[k],
            send_sem=row_send.at[array, k],
            recv_sem=row_recv.at[array, k],
            device_id=(gx + (1 if k == 0 else -1), gy),
            device_id_type=MESH,
        )

    def strip_copy(side, dx):
        return pltpu.make_async_remote_copy(
            src_ref=pack.at[side],
            dst_ref=strips.at[side, 1 - dx],
            send_sem=strip_send.at[side, 1 - dx],
            recv_sem=strip_recv.at[side, 1 - dx],
            device_id=(gx + dx, gy + (1 if side == 0 else -1)),
            device_id_type=MESH,
        )

    loads[0].wait()
    loads[1].wait()
    pl.semaphore_wait(barrier, 4 + n_diag)
    token(0, "tell")
    send_ok = (has_down, has_up)
    recv_ok = (has_up, has_down)
    for k in range(2):
        @pl.when(send_ok[k])
        def _():
            row_copy(1, k).start()
            row_copy(0, k).start()

    half_d = depth // 2

    def place(block, target, first):
        block = block.reshape(half_d, 2, 8, cols)
        for odd in range(2):
            target[first:first + 8, odd * half_d:(odd + 1) * half_d, 0:cols] = jnp.swapaxes(block[:, odd], 0, 1)

    def put_back(source, first, target, row0):
        for odd in range(2):
            block = jnp.swapaxes(source[first:first + 8, odd * half_d:(odd + 1) * half_d, 0:cols], 0, 1)
            for m in range(half_d):
                target[2 * m + odd, row0:row0 + 8, :] = block[m]

    lane = lax.broadcasted_iota(jnp.int32, (depth, 128), 1)
    for part_no in range(rows // 8):
        for source, target in ((in_u, base), (in_k, kap)):
            place(source[:, 8 * part_no:8 * part_no + 8, :], target, lo + 8 * part_no)
    for array, source in enumerate((base, kap)):
        left = jnp.zeros((depth, 128), F32)
        right = jnp.zeros((depth, 128), F32)
        for i in range(rows):
            here = (lane >= 8 * i) & (lane < 8 * i + 8)
            right = jnp.where(here, pltpu.roll(source[lo + i, :, cols - 128:cols], (8 * i + 8) % 128, 1), right)
            first = source[lo + i, :, 0:128]
            left = jnp.where(here, pltpu.roll(first, 8 * i, 1) if i else first, left)
        pack[0, array] = right
        pack[1, array] = left

    side_ok = (has_right, has_left)
    for side in range(2):
        for dx in (0, -1, 1):
            ok = side_ok[side]
            if dx:
                ok = ok & (has_up if dx < 0 else has_down)

            @pl.when(ok)
            def _():
                strip_copy(side, dx).start()

    for k in range(2):
        @pl.when(jnp.logical_not(recv_ok[k]))
        def _():
            halo_u[k] = jnp.zeros(halo_u.shape[1:], F32)
            halo_k[k] = jnp.zeros(halo_k.shape[1:], F32)
    from_ok = (has_left, has_right)
    arrives = {}
    for side in range(2):
        for dx in (0, -1, 1):
            ok = from_ok[side]
            if dx:
                ok = ok & (has_up if dx > 0 else has_down)
            arrives[side, dx] = ok

            @pl.when(jnp.logical_not(ok))
            def _():
                strips[side, 1 - dx] = jnp.zeros(strips.shape[2:], F32)

    loads[3].wait()
    s_of = lax.broadcasted_iota(jnp.int32, (samples, cols), 0)
    c_of = lax.broadcasted_iota(jnp.int32, (samples, cols), 1)
    wanted = jnp.zeros((samples, cols), jnp.int32)
    for s in range(samples):
        wanted = jnp.where(s_of == s, in_cols[s], wanted)
    select = jnp.where(wanted == c_of, 1.0, 0.0).astype(BF16)

    def strips_arrived(dx):
        for side in range(2):
            @pl.when(arrives[side, dx])
            def _():
                strip_copy(side, dx).wait_recv()

    def ring(array, slot, packed_row):
        before = pltpu.roll(strips[0, slot, array], (120 - 8 * packed_row) % 128, 1)
        after = strips[1, slot, array]
        if packed_row:
            after = pltpu.roll(after, (128 - 8 * packed_row) % 128, 1)
        return jnp.where(lane < 8, after, jnp.where(lane >= 120, before, 0.0))

    def close_ring(first, count, slot, packed_row):
        for j in range(count):
            base[first + j, :, cols:wide] = ring(0, slot, packed_row + j)
            kap[first + j, :, cols:wide] = ring(1, slot, packed_row + j)

    middle = (HIGHEST + LOWEST) / 2.0
    spread = (HIGHEST - LOWEST) / 2.0
    ratio = middle / spread
    p_of = lax.broadcasted_iota(jnp.int32, (depth, wide), 0)
    l_of = lax.broadcasted_iota(jnp.int32, (depth, wide), 1)
    at_left, at_right = gy == 0, gy == n_gy - 1
    face_0, face_1 = (l_of == 0) & at_left, (l_of == cols) & at_right
    half_y = jnp.where(face_0 | face_1, 0.0, 0.5)
    half_y2 = jnp.where(((l_of == wide - 1) & at_left) | ((l_of == cols - 1) & at_right), 0.0, 0.5)
    half_z = jnp.where(p_of[0:half_d] == half_d - 1, 0.0, 0.5)
    outer = (
        jnp.where((p_of == 0) | (p_of == depth - 1), 0.5, 0.0)
        + jnp.where(face_0 | ((l_of == cols - 1) & at_right), 0.5, 0.0)
    )

    def face(i):
        fx[i] = 0.5 * (kap[i] + kap[i - 1])

    def coefficients(first, count):
        for i in range(first, first + count):
            here = kap[i]
            even, odd = here[0:half_d], here[half_d:depth]
            fy[i] = half_y * (here + pltpu.roll(here, 1, 1))
            fy2[i] = half_y2 * (here + pltpu.roll(here, wide - 1, 1))
            fz[i, 0:half_d] = 0.5 * (even + odd)
            fz[i, half_d:depth] = half_z * (odd + pltpu.roll(even, half_d - 1, 0))
            diag[i] = REACTION + outer * here
            prec_a[i] = base[i] * (1.0 / middle)

    def applied(source, i, count):
        u = [source[i + j] for j in range(-1, count + 1)]
        flux = [fx[i + j] * (u[j + 1] - u[j]) for j in range(count + 1)]
        for j in range(count):
            here = u[j + 1]
            left = fy[i + j] * (here - pltpu.roll(here, 1, 1))
            right = fy2[i + j] * (pltpu.roll(here, wide - 1, 1) - here)
            out = diag[i + j] * here + (flux[j] - flux[j + 1])
            out = out + (left - right)
            even, odd = here[0:half_d], here[half_d:depth]
            inside = fz[i + j, 0:half_d] * (odd - even)
            between = fz[i + j, half_d:depth] * (pltpu.roll(even, half_d - 1, 0) - odd)
            out_even = out[0:half_d] + (pltpu.roll(between, 1, 0) - inside)
            out_odd = out[half_d:depth] + (inside - between)
            yield j, here, jnp.concatenate([out_even, out_odd], axis=0)

    buffers = (prec_a, prec_b)

    def advance(sweep, i, count):
        keep, gain = weights[sweep]
        source, target = buffers[sweep % 2], buffers[(sweep + 1) % 2]
        for j, here, au in applied(source, i, count):
            change = here if sweep == 0 else here - target[i + j]
            target[i + j] = (here + keep * change) + gain * (base[i + j] - au)

    weights, rho = [], 1.0 / ratio
    for sweep in range(SWEEPS - 1):
        rho_next = 1.0 / (2.0 * ratio - rho)
        weights.append((rho_next * rho, 2.0 * rho_next / spread))
        rho = rho_next

    token(0, "wait")
    token(1, "tell")
    strips_arrived(0)
    close_ring(lo, rows, 1, 0)
    for i in range(lo + 1, hi):
        face(i)
    coefficients(lo, rows)
    for sweep in range(SWEEPS - 1):
        first, end = lo + 1 + sweep, hi - 1 - sweep
        if first < end:
            advance(sweep, first, end - first)
    token(1, "wait")
    token(2, "tell")

    for k, dx, first, packed_row in ((0, 1, 0, rows - HALO), (1, -1, hi, 0)):
        strips_arrived(dx)
        close_ring(first, HALO, 1 - dx, packed_row)

        @pl.when(recv_ok[k])
        def _():
            row_copy(1, k).wait_recv()
            row_copy(0, k).wait_recv()
        for source, target in ((halo_u, base), (halo_k, kap)):
            place(source[k], target, first)
        for i in range(max(first, 1), first + HALO + 1 - k):
            face(i)
        coefficients(first, HALO)
    for inner, edge, ok in ((lo, lo, has_up), (hi - 1, hi, has_down)):
        @pl.when(jnp.logical_not(ok))
        def _():
            fx[edge] = jnp.zeros((depth, wide), F32)
            diag[inner] = diag[inner] + 0.5 * kap[inner]
    for sweep in range(SWEEPS - 1):
        advance(sweep, 1 + sweep, HALO)
        advance(sweep, total - 1 - HALO - sweep, HALO)

    prec = buffers[(SWEEPS - 1) % 2]
    loads[2].wait()

    def last(i, count):
        for j, here, au in applied(prec, i, count):
            own = au[:, 0:cols]
            img[i - lo + j] = own
            flip[i - lo + j] = own * in_sign[pl.ds(i - lo + j, 1), :].astype(F32)

    looped(lo, hi, 8, last)

    high, low = split_bf16(flip[...].reshape(rows * depth, cols))
    picked = dot_nt(select, high) + dot_nt(select, low)
    for q in range(pieces):
        pick[q] = picked[q * share:(q + 1) * share]
    token(2, "wait")
    token(3, "tell")

    def exchange(step, source, target, device):
        return pltpu.make_async_remote_copy(
            src_ref=source, dst_ref=target, send_sem=step_send.at[step], recv_sem=step_recv.at[step],
            device_id=device, device_id_type=MESH,
        )

    for t in far_first(n_gy):
        peer = lax.rem(gy + t, n_gy)
        exchange(0, pick.at[lax.rem(peer, pieces)], recv_1.at[gy], (gx, peer)).start()
    mine = lax.rem(gy, pieces)
    recv_1[gy] = pick[mine]

    for part_no in range(rows // 8):
        put_back(img, 8 * part_no, out_i, 8 * part_no)
    for part_no in range(rows // 8):
        put_back(prec, lo + 8 * part_no, out_p, 8 * part_no)
    stores = [
        pltpu.make_async_copy(source, target, store_sem.at[i])
        for i, (source, target) in enumerate(((out_i, image_hbm), (out_p, prec_hbm), (out_s, sketch_hbm)))
    ]
    stores[0].start()
    stores[1].start()

    others_x, others_y = recv_2.at[pl.ds(0, n_gx - 1)], recv_1.at[pl.ds(0, n_gy - 1)]
    wait_1 = exchange(0, others_y, others_y, (gx, gy))
    wait_1.wait_recv()
    part[...] = jnp.sum(recv_1[...], axis=0)

    token(3, "wait")
    for t in far_in_plane(n_gx):
        exchange(1, part, recv_2.at[gx], around_x(t)).start()
    recv_2[gx] = part[...]
    both = lax.broadcasted_iota(jnp.int32, (n_gx, share, rows * depth), 0) & gx
    parity = jnp.zeros_like(both)
    for bit in range(n_gx.bit_length() - 1):
        parity = parity ^ (both >> bit & 1)
    walsh = (1 - 2 * parity).astype(F32) * (1.0 / n_gx ** 0.5)
    wait_2 = exchange(1, others_x, others_x, (gx, gy))
    wait_2.wait_recv()
    recv_3[mine] = jnp.sum(recv_2[...] * walsh, axis=0)

    near = [t - pieces // 2 for t in range(pieces) if t != pieces // 2]
    for t in sorted(near, key=abs, reverse=True):
        exchange(2, recv_3.at[mine], recv_3.at[mine], around_y(t)).start()
    loads[4].wait()
    wait_3 = None
    if near:
        others_near = recv_1.at[pl.ds(0, pieces - 1)]
        wait_3 = exchange(2, others_near, others_near, (gx, gy))
        wait_3.wait_recv()
    high, low = split_bf16(jnp.concatenate([recv_3[q] for q in range(pieces)], axis=0))
    mixed = dot_nt(in_mix[0], high) + dot_nt(in_mix[0], low) + dot_nt(in_mix[1], high)
    out_s[...] = mixed.reshape(out_s.shape)
    stores[2].start()

    for k in range(2):
        @pl.when(send_ok[k])
        def _():
            row_copy(1, k).wait_send()
            row_copy(0, k).wait_send()
    for side in range(2):
        for dx in (0, -1, 1):
            ok = side_ok[side]
            if dx:
                ok = ok & (has_up if dx < 0 else has_down)

            @pl.when(ok)
            def _():
                strip_copy(side, dx).wait_send()
    wait_1.wait_send()
    wait_2.wait_send()
    if wait_3 is not None:
        wait_3.wait_send()
    for store in stores:
        store.wait()


def hand_on(prec, image, sketch, prec_out, image_out, sketch_out, held_p, held_i, held_s, load_sem, store_sem):
    held = (held_p, held_i, held_s)
    loads = [pltpu.make_async_copy(s, h, load_sem.at[i]) for i, (s, h) in enumerate(zip((prec, image, sketch), held))]
    stores = [
        pltpu.make_async_copy(h, t, store_sem.at[i])
        for i, (h, t) in enumerate(zip(held, (prec_out, image_out, sketch_out)))
    ]
    for load in loads:
        load.start()
    for load, store in zip(loads, stores):
        load.wait()
        store.start()
    for store in stores:
        store.wait()


def per_device(n_gx, n_gy, basis_vec, conductivity, sign_vals, sample_cols):
    depth, rows, cols = basis_vec.shape
    samples = sample_cols.shape[0]
    pieces = max(n_gy // COPIES, 1)
    share = samples // pieces
    wide, total = cols + 128, rows + 2 * HALO
    index = np.arange(rows)
    angle = (index[:, None] * index[None, :] % rows) * (2.0 * np.pi / rows)
    hartley = (np.cos(angle) + np.sin(angle)) / np.sqrt(rows)
    order = np.concatenate([np.arange(0, depth, 2), np.arange(1, depth, 2)])
    mix = np.einsum("jk,de->djke", hartley, np.eye(depth)[:, order]).reshape(depth * rows, rows * depth).astype(np.float32)
    mix_high = mix.astype(jnp.bfloat16)
    mix_low = (mix - mix_high.astype(np.float32)).astype(jnp.bfloat16)
    mix = jnp.asarray(np.stack([mix_high, mix_low]))

    field = (depth, rows, cols)
    tall = pltpu.VMEM((total, depth, wide), F32)
    scratch = [
        pltpu.VMEM(field, F32), pltpu.VMEM(field, F32), pltpu.VMEM((rows, cols), jnp.int32),
        pltpu.SMEM((samples,), jnp.int32), pltpu.VMEM(mix.shape, BF16),
        pltpu.VMEM((2, depth, HALO, cols), F32), pltpu.VMEM((2, depth, HALO, cols), F32),
        pltpu.VMEM((2, 2, depth, 128), F32), pltpu.VMEM((2, 3, 2, depth, 128), F32),
        tall, tall, tall, tall, tall, tall, tall, tall, tall,
        pltpu.VMEM((rows, depth, cols), F32), pltpu.VMEM((rows, depth, cols), F32),
        pltpu.VMEM((pieces, share, rows * depth), F32), pltpu.VMEM((n_gy, share, rows * depth), F32),
        pltpu.VMEM((share, rows * depth), F32), pltpu.VMEM((n_gx, share, rows * depth), F32),
        pltpu.VMEM((pieces, share, rows * depth), F32),
        pltpu.VMEM(field, F32), pltpu.VMEM(field, F32), pltpu.VMEM((depth, rows, samples), F32),
        pltpu.SemaphoreType.DMA((5,)), pltpu.SemaphoreType.DMA((3,)),
        pltpu.SemaphoreType.DMA((2, 2)), pltpu.SemaphoreType.DMA((2, 2)),
        pltpu.SemaphoreType.DMA((2, 3)), pltpu.SemaphoreType.DMA((2, 3)),
        pltpu.SemaphoreType.DMA((3,)), pltpu.SemaphoreType.DMA((3,)),
        pltpu.SemaphoreType.REGULAR((4,)), pltpu.SemaphoreType.REGULAR((4,)),
    ]
    results = pl.pallas_call(
        functools.partial(kernel, n_gx, n_gy),
        out_shape=(
            jax.ShapeDtypeStruct(field, F32),
            jax.ShapeDtypeStruct(field, F32),
            jax.ShapeDtypeStruct((depth, rows, samples), F32),
        ),
        in_specs=[pl.BlockSpec(memory_space=pl.ANY)] * 5,
        out_specs=(pl.BlockSpec(memory_space=pl.ANY),) * 3,
        scratch_shapes=scratch,
        compiler_params=pltpu.CompilerParams(
            collective_id=0, has_side_effects=True, vmem_limit_bytes=59000 * 1024
        ),
    )(basis_vec, conductivity, sign_vals, sample_cols, mix)
    return pl.pallas_call(
        hand_on,
        out_shape=tuple(jax.ShapeDtypeStruct(r.shape, F32) for r in results),
        in_specs=[pl.BlockSpec(memory_space=pl.ANY)] * 3,
        out_specs=(pl.BlockSpec(memory_space=pl.ANY),) * 3,
        scratch_shapes=[pltpu.VMEM(r.shape, F32) for r in results]
        + [pltpu.SemaphoreType.DMA((3,)), pltpu.SemaphoreType.DMA((3,))],
        compiler_params=pltpu.CompilerParams(vmem_limit_bytes=LAST_KIB * 1024),
    )(*results)


def solution(mesh):
    in_specs = (P(None, "gx", "gy"), P(None, "gx", "gy"), P("gx", "gy"), P("gy"))
    out_specs = (P(None, "gx", "gy"), P(None, "gx", "gy"), P(None, "gx", None))
    return jax.shard_map(
        functools.partial(per_device, mesh.shape["gx"], mesh.shape["gy"]),
        mesh=mesh, in_specs=in_specs, out_specs=out_specs, check_vma=False,
    )
```

```python
import functools

import jax
import jax.numpy as jnp
import numpy as np
from jax import lax
from jax.experimental import pallas as pl
from jax.experimental.pallas import tpu as pltpu
from jax.sharding import PartitionSpec as P

SWEEPS = 8
HALO = SWEEPS
REACTION = 0.5
LOWEST = 0.5
HIGHEST = 62.0
MESH = pl.DeviceIdType.MESH
F32 = jnp.float32
BF16 = jnp.bfloat16
COPIES = 4
LAST_KIB = 59000


def far_first(count):
    return sorted(range(1, count), key=lambda t: -min(t, count - t))


def far_in_plane(count):
    def hops(t):
        y, x = t // 2 % 4, t // 8
        return min(y, 4 - y) + min(x, 4 - x)
    return sorted(range(1, count), key=lambda t: -hops(t))


def split_bf16(x):
    high = x.astype(BF16)
    return high, (x - high.astype(F32)).astype(BF16)


def dot_nt(a, b):
    return lax.dot_general(a, b, (((1,), (1,)), ((), ())), preferred_element_type=F32)


def kernel(
    n_gx, n_gy,
    basis_hbm, kappa_hbm, sign_hbm, cols_hbm, mix_hbm,
    prec_hbm, image_hbm, sketch_hbm,
    in_u, in_k, in_sign, in_cols, in_mix,
    halo_u, halo_k, pack, strips,
    kap, fx, fy, fy2, fz, diag, base, prec_a, prec_b, img, flip,
    pick, recv_1, part, recv_2, recv_3, out_p, out_i, out_s,
    load_sem, store_sem, row_send, row_recv, strip_send, strip_recv, step_send, step_recv, token_x, token_y,
):
    depth, rows, cols = in_u.shape
    wide = cols + 128
    lo, hi = HALO, HALO + rows
    total = rows + 2 * HALO
    samples = out_s.shape[2]
    pieces, share = recv_3.shape[0], recv_3.shape[1]
    gx, gy = lax.axis_index("gx"), lax.axis_index("gy")
    has_up, has_down = gx > 0, gx < n_gx - 1
    has_left, has_right = gy > 0, gy < n_gy - 1

    loads = [
        pltpu.make_async_copy(src, dst, load_sem.at[i])
        for i, (src, dst) in enumerate(
            ((basis_hbm, in_u), (kappa_hbm, in_k), (sign_hbm, in_sign), (cols_hbm, in_cols), (mix_hbm, in_mix))
        )
    ]
    for load in loads:
        load.start()

    barrier = pltpu.get_barrier_semaphore()

    def around_x(t):
        return lax.rem(gx + t + n_gx, n_gx), gy

    def around_y(t):
        return gx, lax.rem(gy + t + n_gy, n_gy)

    def tell(semaphore, device):
        pl.semaphore_signal(semaphore, inc=1, device_id=device, device_id_type=MESH)

    for t in (1, -1):
        tell(barrier, around_y(t))
        tell(barrier, around_x(t))
    vertical = ((-1, has_up), (1, has_down))
    sideways = ((-1, has_left), (1, has_right))
    for dx, ok_x in vertical:
        for dy, ok_y in sideways:
            @pl.when(ok_x & ok_y)
            def _():
                tell(barrier, (gx + dx, gy + dy))
    n_diag = (has_up.astype(jnp.int32) + has_down.astype(jnp.int32)) * (
        has_left.astype(jnp.int32) + has_right.astype(jnp.int32)
    )

    rings = {"x": (n_gx, around_x, token_x), "y": (n_gy, around_y, token_y)}

    def token(ring_name, round_no, action):
        count, around, semaphores = rings[ring_name]
        distance = 1 << round_no
        if distance < count // 2:
            if action == "tell":
                tell(semaphores.at[round_no], around(distance))
                tell(semaphores.at[round_no], around(-distance))
            else:
                pl.semaphore_wait(semaphores.at[round_no], 2)

    def row_copy(array, k):
        source, target = ((in_u, halo_u), (in_k, halo_k))[array]
        first = rows - HALO if k == 0 else 0
        return pltpu.make_async_remote_copy(
            src_ref=source.at[:, pl.ds(first, HALO), :],
            dst_ref=target.at[k],
            send_sem=row_send.at[array, k],
            recv_sem=row_recv.at[array, k],
            device_id=(gx + (1 if k == 0 else -1), gy),
            device_id_type=MESH,
        )

    def strip_copy(side, dx):
        return pltpu.make_async_remote_copy(
            src_ref=pack.at[side],
            dst_ref=strips.at[side, 1 - dx],
            send_sem=strip_send.at[side, 1 - dx],
            recv_sem=strip_recv.at[side, 1 - dx],
            device_id=(gx + dx, gy + (1 if side == 0 else -1)),
            device_id_type=MESH,
        )

    loads[0].wait()
    loads[1].wait()
    half_d = depth // 2

    def place(block, target, first):
        block = block.reshape(half_d, 2, 8, cols)
        for odd in range(2):
            target[first:first + 8, odd * half_d:(odd + 1) * half_d, 0:cols] = jnp.swapaxes(block[:, odd], 0, 1)

    def put_back(source, first, target, row0):
        for odd in range(2):
            block = jnp.swapaxes(source[first:first + 8, odd * half_d:(odd + 1) * half_d, 0:cols], 0, 1)
            for m in range(half_d):
                target[2 * m + odd, row0:row0 + 8, :] = block[m]

    lane = lax.broadcasted_iota(jnp.int32, (depth, 128), 1)
    for part_no in range(rows // 8):
        for source, target in ((in_u, base), (in_k, kap)):
            place(source[:, 8 * part_no:8 * part_no + 8, :], target, lo + 8 * part_no)
    for array, source in enumerate((base, kap)):
        left = jnp.zeros((depth, 128), F32)
        right = jnp.zeros((depth, 128), F32)
        for i in range(rows):
            here = (lane >= 8 * i) & (lane < 8 * i + 8)
            right = jnp.where(here, pltpu.roll(source[lo + i, :, cols - 128:cols], (8 * i + 8) % 128, 1), right)
            first = source[lo + i, :, 0:128]
            left = jnp.where(here, pltpu.roll(first, 8 * i, 1) if i else first, left)
        pack[0, array] = right
        pack[1, array] = left

    pl.semaphore_wait(barrier, 4 + n_diag)
    token("y", 0, "tell")
    token("x", 0, "tell")
    side_ok = (has_right, has_left)
    for side in range(2):
        for dx in (0, -1, 1):
            ok = side_ok[side]
            if dx:
                ok = ok & (has_up if dx < 0 else has_down)

            @pl.when(ok)
            def _():
                strip_copy(side, dx).start()

    send_ok = (has_down, has_up)
    recv_ok = (has_up, has_down)
    for k in range(2):
        @pl.when(send_ok[k])
        def _():
            row_copy(1, k).start()
            row_copy(0, k).start()

    for k in range(2):
        @pl.when(jnp.logical_not(recv_ok[k]))
        def _():
            halo_u[k] = jnp.zeros(halo_u.shape[1:], F32)
            halo_k[k] = jnp.zeros(halo_k.shape[1:], F32)
    from_ok = (has_left, has_right)
    arrives = {}
    for side in range(2):
        for dx in (0, -1, 1):
            ok = from_ok[side]
            if dx:
                ok = ok & (has_up if dx > 0 else has_down)
            arrives[side, dx] = ok

            @pl.when(jnp.logical_not(ok))
            def _():
                strips[side, 1 - dx] = jnp.zeros(strips.shape[2:], F32)

    loads[3].wait()
    s_of = lax.broadcasted_iota(jnp.int32, (samples, cols), 0)
    c_of = lax.broadcasted_iota(jnp.int32, (samples, cols), 1)
    wanted = jnp.zeros((samples, cols), jnp.int32)
    for s in range(samples):
        wanted = jnp.where(s_of == s, in_cols[s], wanted)
    select = jnp.where(wanted == c_of, 1.0, 0.0).astype(BF16)

    def strips_arrived(dx):
        for side in range(2):
            @pl.when(arrives[side, dx])
            def _():
                strip_copy(side, dx).wait_recv()

    def ring(array, slot, packed_row):
        before = pltpu.roll(strips[0, slot, array], (120 - 8 * packed_row) % 128, 1)
        after = strips[1, slot, array]
        if packed_row:
            after = pltpu.roll(after, (128 - 8 * packed_row) % 128, 1)
        return jnp.where(lane < 8, after, jnp.where(lane >= 120, before, 0.0))

    def close_ring(first, count, slot, packed_row):
        for j in range(count):
            base[first + j, :, cols:wide] = ring(0, slot, packed_row + j)
            kap[first + j, :, cols:wide] = ring(1, slot, packed_row + j)

    middle = (HIGHEST + LOWEST) / 2.0
    spread = (HIGHEST - LOWEST) / 2.0
    ratio = middle / spread
    p_of = lax.broadcasted_iota(jnp.int32, (depth, wide), 0)
    l_of = lax.broadcasted_iota(jnp.int32, (depth, wide), 1)
    at_left, at_right = gy == 0, gy == n_gy - 1
    face_0, face_1 = (l_of == 0) & at_left, (l_of == cols) & at_right
    half_y = jnp.where(face_0 | face_1, 0.0, 0.5)
    half_y2 = jnp.where(((l_of == wide - 1) & at_left) | ((l_of == cols - 1) & at_right), 0.0, 0.5)
    half_z = jnp.where(p_of[0:half_d] == half_d - 1, 0.0, 0.5)
    outer = (
        jnp.where((p_of == 0) | (p_of == depth - 1), 0.5, 0.0)
        + jnp.where(face_0 | ((l_of == cols - 1) & at_right), 0.5, 0.0)
    )

    def face(i):
        fx[i] = 0.5 * (kap[i] + kap[i - 1])

    def coefficients(first, count):
        for i in range(first, first + count):
            here = kap[i]
            even, odd = here[0:half_d], here[half_d:depth]
            fy[i] = half_y * (here + pltpu.roll(here, 1, 1))
            fy2[i] = half_y2 * (here + pltpu.roll(here, wide - 1, 1))
            fz[i, 0:half_d] = 0.5 * (even + odd)
            fz[i, half_d:depth] = half_z * (odd + pltpu.roll(even, half_d - 1, 0))
            diag[i] = REACTION + outer * here
            prec_a[i] = base[i] * (1.0 / middle)

    def applied(source, i, count):
        u = [source[i + j] for j in range(-1, count + 1)]
        flux = [fx[i + j] * (u[j + 1] - u[j]) for j in range(count + 1)]
        for j in range(count):
            here = u[j + 1]
            left = fy[i + j] * (here - pltpu.roll(here, 1, 1))
            right = fy2[i + j] * (pltpu.roll(here, wide - 1, 1) - here)
            out = diag[i + j] * here + (flux[j] - flux[j + 1])
            out = out + (left - right)
            even, odd = here[0:half_d], here[half_d:depth]
            inside = fz[i + j, 0:half_d] * (odd - even)
            between = fz[i + j, half_d:depth] * (pltpu.roll(even, half_d - 1, 0) - odd)
            out_even = out[0:half_d] + (pltpu.roll(between, 1, 0) - inside)
            out_odd = out[half_d:depth] + (inside - between)
            yield j, here, jnp.concatenate([out_even, out_odd], axis=0)

    buffers = (prec_a, prec_b)

    def advance(sweep, i, count):
        keep, gain = weights[sweep]
        source, target = buffers[sweep % 2], buffers[(sweep + 1) % 2]
        for j, here, au in applied(source, i, count):
            change = here if sweep == 0 else here - target[i + j]
            target[i + j] = (here + keep * change) + gain * (base[i + j] - au)

    weights, rho = [], 1.0 / ratio
    for sweep in range(SWEEPS - 1):
        rho_next = 1.0 / (2.0 * ratio - rho)
        weights.append((rho_next * rho, 2.0 * rho_next / spread))
        rho = rho_next

    token("y", 0, "wait")
    token("y", 1, "tell")
    strips_arrived(0)
    close_ring(lo, rows, 1, 0)
    for i in range(lo + 1, hi):
        face(i)
    coefficients(lo, rows)
    for sweep in range(SWEEPS - 1):
        first, end = lo + 1 + sweep, hi - 1 - sweep
        if first < end:
            advance(sweep, first, end - first)
    token("y", 1, "wait")
    token("y", 2, "tell")
    token("x", 0, "wait")
    token("x", 1, "tell")

    for k, dx, first, packed_row in ((0, 1, 0, rows - HALO), (1, -1, hi, 0)):
        strips_arrived(dx)
        close_ring(first, HALO, 1 - dx, packed_row)

        @pl.when(recv_ok[k])
        def _():
            row_copy(1, k).wait_recv()
            row_copy(0, k).wait_recv()
        for source, target in ((halo_u, base), (halo_k, kap)):
            place(source[k], target, first)
        for i in range(max(first, 1), first + HALO + 1 - k):
            face(i)
        coefficients(first, HALO)
    for inner, edge, ok in ((lo, lo, has_up), (hi - 1, hi, has_down)):
        @pl.when(jnp.logical_not(ok))
        def _():
            fx[edge] = jnp.zeros((depth, wide), F32)
            diag[inner] = diag[inner] + 0.5 * kap[inner]
    for sweep in range(SWEEPS - 1):
        advance(sweep, 1 + sweep, HALO)
        advance(sweep, total - 1 - HALO - sweep, HALO)

    prec = buffers[(SWEEPS - 1) % 2]
    loads[2].wait()

    picked = []
    for first in range(lo, hi, 8):
        for j, here, au in applied(prec, first, 8):
            i = first - lo + j
            own = au[:, 0:cols]
            img[i] = own
            flip[i] = own * in_sign[i:i + 1, :].astype(F32)
        high, low = split_bf16(flip[first - lo:first - lo + 8].reshape(8 * depth, cols))
        picked.append(dot_nt(select, high) + dot_nt(select, low))
    picked = jnp.concatenate(picked, axis=1)
    for q in range(pieces):
        pick[q] = picked[q * share:(q + 1) * share]
    token("y", 2, "wait")

    def exchange(step, source, target, device):
        return pltpu.make_async_remote_copy(
            src_ref=source, dst_ref=target, send_sem=step_send.at[step], recv_sem=step_recv.at[step],
            device_id=device, device_id_type=MESH,
        )

    for t in far_first(n_gy):
        peer = lax.rem(gy + t, n_gy)
        exchange(0, pick.at[lax.rem(peer, pieces)], recv_1.at[gy], (gx, peer)).start()
    mine = lax.rem(gy, pieces)
    recv_1[gy] = pick[mine]
    token("x", 1, "wait")
    token("x", 2, "tell")

    for part_no in range(rows // 8):
        put_back(img, 8 * part_no, out_i, 8 * part_no)
    for part_no in range(rows // 8):
        put_back(prec, lo + 8 * part_no, out_p, 8 * part_no)
    stores = [
        pltpu.make_async_copy(source, target, store_sem.at[i])
        for i, (source, target) in enumerate(((out_i, image_hbm), (out_p, prec_hbm), (out_s, sketch_hbm)))
    ]
    stores[0].start()
    stores[1].start()

    token("x", 2, "wait")
    token("x", 3, "tell")

    others_x, others_y = recv_2.at[pl.ds(0, n_gx - 1)], recv_1.at[pl.ds(0, n_gy - 1)]
    wait_1 = exchange(0, others_y, others_y, (gx, gy))
    wait_1.wait_recv()
    part[...] = jnp.sum(recv_1[...], axis=0)

    token("x", 3, "wait")
    for t in far_in_plane(n_gx):
        exchange(1, part, recv_2.at[gx], around_x(t)).start()
    recv_2[gx] = part[...]
    both = lax.broadcasted_iota(jnp.int32, (n_gx, share, rows * depth), 0) & gx
    parity = jnp.zeros_like(both)
    for bit in range(n_gx.bit_length() - 1):
        parity = parity ^ (both >> bit & 1)
    walsh = (1 - 2 * parity).astype(F32) * (1.0 / n_gx ** 0.5)
    wait_2 = exchange(1, others_x, others_x, (gx, gy))
    wait_2.wait_recv()
    recv_3[mine] = jnp.sum(recv_2[...] * walsh, axis=0)

    near = [t - pieces // 2 for t in range(pieces) if t != pieces // 2]
    for t in sorted(near, key=abs, reverse=True):
        exchange(2, recv_3.at[mine], recv_3.at[mine], around_y(t)).start()
    loads[4].wait()
    wait_3 = None
    if near:
        others_near = recv_1.at[pl.ds(0, pieces - 1)]
        wait_3 = exchange(2, others_near, others_near, (gx, gy))
        wait_3.wait_recv()
    high, low = split_bf16(jnp.concatenate([recv_3[q] for q in range(pieces)], axis=0))
    mixed = dot_nt(in_mix[0], high) + dot_nt(in_mix[0], low) + dot_nt(in_mix[1], high)
    out_s[...] = mixed.reshape(out_s.shape)
    stores[2].start()

    for k in range(2):
        @pl.when(send_ok[k])
        def _():
            row_copy(1, k).wait_send()
            row_copy(0, k).wait_send()
    for side in range(2):
        for dx in (0, -1, 1):
            ok = side_ok[side]
            if dx:
                ok = ok & (has_up if dx < 0 else has_down)

            @pl.when(ok)
            def _():
                strip_copy(side, dx).wait_send()
    wait_1.wait_send()
    wait_2.wait_send()
    if wait_3 is not None:
        wait_3.wait_send()
    for store in stores:
        store.wait()


def hand_on(prec, image, sketch, prec_out, image_out, sketch_out, held_p, held_i, held_s, load_sem, store_sem):
    held = (held_p, held_i, held_s)
    loads = [pltpu.make_async_copy(s, h, load_sem.at[i]) for i, (s, h) in enumerate(zip((prec, image, sketch), held))]
    stores = [
        pltpu.make_async_copy(h, t, store_sem.at[i])
        for i, (h, t) in enumerate(zip(held, (prec_out, image_out, sketch_out)))
    ]
    for load in loads:
        load.start()
    for load, store in zip(loads, stores):
        load.wait()
        store.start()
    for store in stores:
        store.wait()


def per_device(n_gx, n_gy, basis_vec, conductivity, sign_vals, sample_cols):
    depth, rows, cols = basis_vec.shape
    samples = sample_cols.shape[0]
    pieces = max(n_gy // COPIES, 1)
    share = samples // pieces
    wide, total = cols + 128, rows + 2 * HALO
    index = np.arange(rows)
    angle = (index[:, None] * index[None, :] % rows) * (2.0 * np.pi / rows)
    hartley = (np.cos(angle) + np.sin(angle)) / np.sqrt(rows)
    order = np.concatenate([np.arange(0, depth, 2), np.arange(1, depth, 2)])
    mix = np.einsum("jk,de->djke", hartley, np.eye(depth)[:, order]).reshape(depth * rows, rows * depth).astype(np.float32)
    mix_high = mix.astype(jnp.bfloat16)
    mix_low = (mix - mix_high.astype(np.float32)).astype(jnp.bfloat16)
    mix = jnp.asarray(np.stack([mix_high, mix_low]))

    field = (depth, rows, cols)
    tall = pltpu.VMEM((total, depth, wide), F32)
    scratch = [
        pltpu.VMEM(field, F32), pltpu.VMEM(field, F32), pltpu.VMEM((rows, cols), jnp.int32),
        pltpu.SMEM((samples,), jnp.int32), pltpu.VMEM(mix.shape, BF16),
        pltpu.VMEM((2, depth, HALO, cols), F32), pltpu.VMEM((2, depth, HALO, cols), F32),
        pltpu.VMEM((2, 2, depth, 128), F32), pltpu.VMEM((2, 3, 2, depth, 128), F32),
        tall, tall, tall, tall, tall, tall, tall, tall, tall,
        pltpu.VMEM((rows, depth, cols), F32), pltpu.VMEM((rows, depth, cols), F32),
        pltpu.VMEM((pieces, share, rows * depth), F32), pltpu.VMEM((n_gy, share, rows * depth), F32),
        pltpu.VMEM((share, rows * depth), F32), pltpu.VMEM((n_gx, share, rows * depth), F32),
        pltpu.VMEM((pieces, share, rows * depth), F32),
        pltpu.VMEM(field, F32), pltpu.VMEM(field, F32), pltpu.VMEM((depth, rows, samples), F32),
        pltpu.SemaphoreType.DMA((5,)), pltpu.SemaphoreType.DMA((3,)),
        pltpu.SemaphoreType.DMA((2, 2)), pltpu.SemaphoreType.DMA((2, 2)),
        pltpu.SemaphoreType.DMA((2, 3)), pltpu.SemaphoreType.DMA((2, 3)),
        pltpu.SemaphoreType.DMA((3,)), pltpu.SemaphoreType.DMA((3,)),
        pltpu.SemaphoreType.REGULAR((4,)), pltpu.SemaphoreType.REGULAR((4,)),
    ]
    results = pl.pallas_call(
        functools.partial(kernel, n_gx, n_gy),
        out_shape=(
            jax.ShapeDtypeStruct(field, F32),
            jax.ShapeDtypeStruct(field, F32),
            jax.ShapeDtypeStruct((depth, rows, samples), F32),
        ),
        in_specs=[pl.BlockSpec(memory_space=pl.ANY)] * 5,
        out_specs=(pl.BlockSpec(memory_space=pl.ANY),) * 3,
        scratch_shapes=scratch,
        compiler_params=pltpu.CompilerParams(
            collective_id=0, has_side_effects=True, vmem_limit_bytes=59000 * 1024
        ),
    )(basis_vec, conductivity, sign_vals, sample_cols, mix)
    return pl.pallas_call(
        hand_on,
        out_shape=tuple(jax.ShapeDtypeStruct(r.shape, F32) for r in results),
        in_specs=[pl.BlockSpec(memory_space=pl.ANY)] * 3,
        out_specs=(pl.BlockSpec(memory_space=pl.ANY),) * 3,
        scratch_shapes=[pltpu.VMEM(r.shape, F32) for r in results]
        + [pltpu.SemaphoreType.DMA((3,)), pltpu.SemaphoreType.DMA((3,))],
        compiler_params=pltpu.CompilerParams(vmem_limit_bytes=LAST_KIB * 1024),
    )(*results)


def solution(mesh):
    in_specs = (P(None, "gx", "gy"), P(None, "gx", "gy"), P("gx", "gy"), P("gy"))
    out_specs = (P(None, "gx", "gy"), P(None, "gx", "gy"), P(None, "gx", None))
    return jax.shard_map(
        functools.partial(per_device, mesh.shape["gx"], mesh.shape["gy"]),
        mesh=mesh, in_specs=in_specs, out_specs=out_specs, check_vma=False,
    )
```

```python
import functools

import jax
import jax.numpy as jnp
import numpy as np
from jax import lax
from jax.experimental import pallas as pl
from jax.experimental.pallas import tpu as pltpu
from jax.sharding import PartitionSpec as P

SWEEPS = 8
HALO = SWEEPS
REACTION = 0.5
LOWEST = 0.5
HIGHEST = 62.0
MESH = pl.DeviceIdType.MESH
F32 = jnp.float32
BF16 = jnp.bfloat16
COPIES = 4
LAST_KIB = 59000
HAND_ON_PARTS = 2


def far_first(count):
    return sorted(range(1, count), key=lambda t: -min(t, count - t))


def far_in_plane(count):
    def hops(t):
        y, x = t // 2 % 4, t // 8
        return min(y, 4 - y) + min(x, 4 - x)
    return sorted(range(1, count), key=lambda t: -hops(t))


def split_bf16(x):
    high = x.astype(BF16)
    return high, (x - high.astype(F32)).astype(BF16)


def dot_nt(a, b):
    return lax.dot_general(a, b, (((1,), (1,)), ((), ())), preferred_element_type=F32)


def kernel(
    n_gx, n_gy,
    basis_hbm, kappa_hbm, sign_hbm, cols_hbm, mix_hbm,
    prec_hbm, image_hbm, sketch_hbm,
    in_u, in_k, in_sign, in_cols, in_mix,
    halo_u, halo_k, pack, strips,
    kap, fx, fy, fy2, fz, diag, base, prec_a, prec_b, img, flip,
    pick, recv_1, part, recv_2, recv_3, out_p, out_i, out_s,
    load_sem, store_sem, row_send, row_recv, strip_send, strip_recv, step_send, step_recv, token_x, token_y,
):
    depth, rows, cols = in_u.shape
    wide = cols + 128
    lo, hi = HALO, HALO + rows
    total = rows + 2 * HALO
    samples = out_s.shape[2]
    pieces, share = recv_3.shape[0], recv_3.shape[1]
    gx, gy = lax.axis_index("gx"), lax.axis_index("gy")
    has_up, has_down = gx > 0, gx < n_gx - 1
    has_left, has_right = gy > 0, gy < n_gy - 1

    loads = [
        pltpu.make_async_copy(src, dst, load_sem.at[i])
        for i, (src, dst) in enumerate(
            ((basis_hbm, in_u), (kappa_hbm, in_k), (sign_hbm, in_sign), (cols_hbm, in_cols), (mix_hbm, in_mix))
        )
    ]
    for load in loads:
        load.start()

    barrier = pltpu.get_barrier_semaphore()

    def around_x(t):
        return lax.rem(gx + t + n_gx, n_gx), gy

    def around_y(t):
        return gx, lax.rem(gy + t + n_gy, n_gy)

    def tell(semaphore, device):
        pl.semaphore_signal(semaphore, inc=1, device_id=device, device_id_type=MESH)

    for t in (1, -1):
        tell(barrier, around_y(t))
        tell(barrier, around_x(t))
    vertical = ((-1, has_up), (1, has_down))
    sideways = ((-1, has_left), (1, has_right))
    for dx, ok_x in vertical:
        for dy, ok_y in sideways:
            @pl.when(ok_x & ok_y)
            def _():
                tell(barrier, (gx + dx, gy + dy))
    n_diag = (has_up.astype(jnp.int32) + has_down.astype(jnp.int32)) * (
        has_left.astype(jnp.int32) + has_right.astype(jnp.int32)
    )

    rings = {"x": (n_gx, around_x, token_x), "y": (n_gy, around_y, token_y)}

    def token(ring_name, round_no, action):
        count, around, semaphores = rings[ring_name]
        distance = 1 << round_no
        if distance < count // 2:
            if action == "tell":
                tell(semaphores.at[round_no], around(distance))
                tell(semaphores.at[round_no], around(-distance))
            else:
                pl.semaphore_wait(semaphores.at[round_no], 2)

    def row_copy(array, k):
        source, target = ((in_u, halo_u), (in_k, halo_k))[array]
        first = rows - HALO if k == 0 else 0
        return pltpu.make_async_remote_copy(
            src_ref=source.at[:, pl.ds(first, HALO), :],
            dst_ref=target.at[k],
            send_sem=row_send.at[array, k],
            recv_sem=row_recv.at[array, k],
            device_id=(gx + (1 if k == 0 else -1), gy),
            device_id_type=MESH,
        )

    def strip_copy(side, dx):
        return pltpu.make_async_remote_copy(
            src_ref=pack.at[side],
            dst_ref=strips.at[side, 1 - dx],
            send_sem=strip_send.at[side, 1 - dx],
            recv_sem=strip_recv.at[side, 1 - dx],
            device_id=(gx + dx, gy + (1 if side == 0 else -1)),
            device_id_type=MESH,
        )

    loads[0].wait()
    loads[1].wait()
    half_d = depth // 2

    def place(block, target, first):
        block = block.reshape(half_d, 2, 8, cols)
        for odd in range(2):
            target[first:first + 8, odd * half_d:(odd + 1) * half_d, 0:cols] = jnp.swapaxes(block[:, odd], 0, 1)

    def put_back(source, first, target, row0):
        for odd in range(2):
            block = jnp.swapaxes(source[first:first + 8, odd * half_d:(odd + 1) * half_d, 0:cols], 0, 1)
            for m in range(half_d):
                target[2 * m + odd, row0:row0 + 8, :] = block[m]

    lane = lax.broadcasted_iota(jnp.int32, (depth, 128), 1)
    for part_no in range(rows // 8):
        for source, target in ((in_u, base), (in_k, kap)):
            place(source[:, 8 * part_no:8 * part_no + 8, :], target, lo + 8 * part_no)
    for array, source in enumerate((base, kap)):
        left = jnp.zeros((depth, 128), F32)
        right = jnp.zeros((depth, 128), F32)
        for i in range(rows):
            here = (lane >= 8 * i) & (lane < 8 * i + 8)
            right = jnp.where(here, pltpu.roll(source[lo + i, :, cols - 128:cols], (8 * i + 8) % 128, 1), right)
            first = source[lo + i, :, 0:128]
            left = jnp.where(here, pltpu.roll(first, 8 * i, 1) if i else first, left)
        pack[0, array] = right
        pack[1, array] = left

    pl.semaphore_wait(barrier, 4 + n_diag)
    token("y", 0, "tell")
    token("x", 0, "tell")
    side_ok = (has_right, has_left)
    for side in range(2):
        for dx in (0, -1, 1):
            ok = side_ok[side]
            if dx:
                ok = ok & (has_up if dx < 0 else has_down)

            @pl.when(ok)
            def _():
                strip_copy(side, dx).start()

    send_ok = (has_down, has_up)
    recv_ok = (has_up, has_down)
    for k in range(2):
        @pl.when(send_ok[k])
        def _():
            row_copy(1, k).start()
            row_copy(0, k).start()

    for k in range(2):
        @pl.when(jnp.logical_not(recv_ok[k]))
        def _():
            halo_u[k] = jnp.zeros(halo_u.shape[1:], F32)
            halo_k[k] = jnp.zeros(halo_k.shape[1:], F32)
    from_ok = (has_left, has_right)
    arrives = {}
    for side in range(2):
        for dx in (0, -1, 1):
            ok = from_ok[side]
            if dx:
                ok = ok & (has_up if dx > 0 else has_down)
            arrives[side, dx] = ok

            @pl.when(jnp.logical_not(ok))
            def _():
                strips[side, 1 - dx] = jnp.zeros(strips.shape[2:], F32)

    loads[3].wait()
    s_of = lax.broadcasted_iota(jnp.int32, (samples, cols), 0)
    c_of = lax.broadcasted_iota(jnp.int32, (samples, cols), 1)
    wanted = jnp.zeros((samples, cols), jnp.int32)
    for s in range(samples):
        wanted = jnp.where(s_of == s, in_cols[s], wanted)
    select = jnp.where(wanted == c_of, 1.0, 0.0).astype(BF16)

    def strips_arrived(dx):
        for side in range(2):
            @pl.when(arrives[side, dx])
            def _():
                strip_copy(side, dx).wait_recv()

    def ring(array, slot, packed_row):
        before = pltpu.roll(strips[0, slot, array], (120 - 8 * packed_row) % 128, 1)
        after = strips[1, slot, array]
        if packed_row:
            after = pltpu.roll(after, (128 - 8 * packed_row) % 128, 1)
        return jnp.where(lane < 8, after, jnp.where(lane >= 120, before, 0.0))

    def close_ring(first, count, slot, packed_row):
        for j in range(count):
            base[first + j, :, cols:wide] = ring(0, slot, packed_row + j)
            kap[first + j, :, cols:wide] = ring(1, slot, packed_row + j)

    middle = (HIGHEST + LOWEST) / 2.0
    spread = (HIGHEST - LOWEST) / 2.0
    ratio = middle / spread
    p_of = lax.broadcasted_iota(jnp.int32, (depth, wide), 0)
    l_of = lax.broadcasted_iota(jnp.int32, (depth, wide), 1)
    at_left, at_right = gy == 0, gy == n_gy - 1
    face_0, face_1 = (l_of == 0) & at_left, (l_of == cols) & at_right
    half_y = jnp.where(face_0 | face_1, 0.0, 0.5)
    half_y2 = jnp.where(((l_of == wide - 1) & at_left) | ((l_of == cols - 1) & at_right), 0.0, 0.5)
    half_z = jnp.where(p_of[0:half_d] == half_d - 1, 0.0, 0.5)
    outer = (
        jnp.where((p_of == 0) | (p_of == depth - 1), 0.5, 0.0)
        + jnp.where(face_0 | ((l_of == cols - 1) & at_right), 0.5, 0.0)
    )

    def face(i):
        fx[i] = 0.5 * (kap[i] + kap[i - 1])

    def coefficients(first, count):
        for i in range(first, first + count):
            here = kap[i]
            even, odd = here[0:half_d], here[half_d:depth]
            fy[i] = half_y * (here + pltpu.roll(here, 1, 1))
            fy2[i] = half_y2 * (here + pltpu.roll(here, wide - 1, 1))
            fz[i, 0:half_d] = 0.5 * (even + odd)
            fz[i, half_d:depth] = half_z * (odd + pltpu.roll(even, half_d - 1, 0))
            diag[i] = REACTION + outer * here
            prec_a[i] = base[i] * (1.0 / middle)

    def applied(source, i, count):
        u = [source[i + j] for j in range(-1, count + 1)]
        flux = [fx[i + j] * (u[j + 1] - u[j]) for j in range(count + 1)]
        for j in range(count):
            here = u[j + 1]
            left = fy[i + j] * (here - pltpu.roll(here, 1, 1))
            right = fy2[i + j] * (pltpu.roll(here, wide - 1, 1) - here)
            out = diag[i + j] * here + (flux[j] - flux[j + 1])
            out = out + (left - right)
            even, odd = here[0:half_d], here[half_d:depth]
            inside = fz[i + j, 0:half_d] * (odd - even)
            between = fz[i + j, half_d:depth] * (pltpu.roll(even, half_d - 1, 0) - odd)
            out_even = out[0:half_d] + (pltpu.roll(between, 1, 0) - inside)
            out_odd = out[half_d:depth] + (inside - between)
            yield j, here, jnp.concatenate([out_even, out_odd], axis=0)

    buffers = (prec_a, prec_b)

    def advance(sweep, i, count):
        keep, gain = weights[sweep]
        source, target = buffers[sweep % 2], buffers[(sweep + 1) % 2]
        for j, here, au in applied(source, i, count):
            change = here if sweep == 0 else here - target[i + j]
            target[i + j] = (here + keep * change) + gain * (base[i + j] - au)

    weights, rho = [], 1.0 / ratio
    for sweep in range(SWEEPS - 1):
        rho_next = 1.0 / (2.0 * ratio - rho)
        weights.append((rho_next * rho, 2.0 * rho_next / spread))
        rho = rho_next

    token("y", 0, "wait")
    token("y", 1, "tell")
    strips_arrived(0)
    close_ring(lo, rows, 1, 0)
    for i in range(lo + 1, hi):
        face(i)
    coefficients(lo, rows)
    for sweep in range(SWEEPS - 1):
        first, end = lo + 1 + sweep, hi - 1 - sweep
        if first < end:
            advance(sweep, first, end - first)
    token("y", 1, "wait")
    token("y", 2, "tell")
    token("x", 0, "wait")
    token("x", 1, "tell")

    for k, dx, first, packed_row in ((0, 1, 0, rows - HALO), (1, -1, hi, 0)):
        strips_arrived(dx)
        close_ring(first, HALO, 1 - dx, packed_row)

        @pl.when(recv_ok[k])
        def _():
            row_copy(1, k).wait_recv()
            row_copy(0, k).wait_recv()
        for source, target in ((halo_u, base), (halo_k, kap)):
            place(source[k], target, first)
        for i in range(max(first, 1), first + HALO + 1 - k):
            face(i)
        coefficients(first, HALO)
    for inner, edge, ok in ((lo, lo, has_up), (hi - 1, hi, has_down)):
        @pl.when(jnp.logical_not(ok))
        def _():
            fx[edge] = jnp.zeros((depth, wide), F32)
            diag[inner] = diag[inner] + 0.5 * kap[inner]
    for sweep in range(SWEEPS - 1):
        advance(sweep, 1 + sweep, HALO)
        advance(sweep, total - 1 - HALO - sweep, HALO)

    prec = buffers[(SWEEPS - 1) % 2]
    loads[2].wait()

    picked = []
    for first in range(lo, hi, 8):
        for j, here, au in applied(prec, first, 8):
            i = first - lo + j
            own = au[:, 0:cols]
            img[i] = own
            flip[i] = own * in_sign[i:i + 1, :].astype(F32)
        high, low = split_bf16(flip[first - lo:first - lo + 8].reshape(8 * depth, cols))
        picked.append(dot_nt(select, high) + dot_nt(select, low))
    picked = jnp.concatenate(picked, axis=1)
    for q in range(pieces):
        pick[q] = picked[q * share:(q + 1) * share]
    token("y", 2, "wait")

    def exchange(step, source, target, device):
        return pltpu.make_async_remote_copy(
            src_ref=source, dst_ref=target, send_sem=step_send.at[step], recv_sem=step_recv.at[step],
            device_id=device, device_id_type=MESH,
        )

    for t in far_first(n_gy):
        peer = lax.rem(gy + t, n_gy)
        exchange(0, pick.at[lax.rem(peer, pieces)], recv_1.at[gy], (gx, peer)).start()
    mine = lax.rem(gy, pieces)
    recv_1[gy] = pick[mine]
    token("x", 1, "wait")
    token("x", 2, "tell")

    for part_no in range(rows // 8):
        put_back(img, 8 * part_no, out_i, 8 * part_no)
    for part_no in range(rows // 8):
        put_back(prec, lo + 8 * part_no, out_p, 8 * part_no)
    stores = [
        pltpu.make_async_copy(source, target, store_sem.at[i])
        for i, (source, target) in enumerate(((out_i, image_hbm), (out_p, prec_hbm), (out_s, sketch_hbm)))
    ]
    stores[0].start()
    stores[1].start()

    token("x", 2, "wait")
    token("x", 3, "tell")

    others_x, others_y = recv_2.at[pl.ds(0, n_gx - 1)], recv_1.at[pl.ds(0, n_gy - 1)]
    wait_1 = exchange(0, others_y, others_y, (gx, gy))
    wait_1.wait_recv()
    part[...] = jnp.sum(recv_1[...], axis=0)

    token("x", 3, "wait")
    for t in far_in_plane(n_gx):
        exchange(1, part, recv_2.at[gx], around_x(t)).start()
    recv_2[gx] = part[...]
    both = lax.broadcasted_iota(jnp.int32, (n_gx, share, rows * depth), 0) & gx
    parity = jnp.zeros_like(both)
    for bit in range(n_gx.bit_length() - 1):
        parity = parity ^ (both >> bit & 1)
    walsh = (1 - 2 * parity).astype(F32) * (1.0 / n_gx ** 0.5)
    wait_2 = exchange(1, others_x, others_x, (gx, gy))
    wait_2.wait_recv()
    recv_3[mine] = jnp.sum(recv_2[...] * walsh, axis=0)

    near = [t - pieces // 2 for t in range(pieces) if t != pieces // 2]
    for t in sorted(near, key=abs, reverse=True):
        exchange(2, recv_3.at[mine], recv_3.at[mine], around_y(t)).start()
    loads[4].wait()
    wait_3 = None
    if near:
        others_near = recv_1.at[pl.ds(0, pieces - 1)]
        wait_3 = exchange(2, others_near, others_near, (gx, gy))
        wait_3.wait_recv()
    high, low = split_bf16(jnp.concatenate([recv_3[q] for q in range(pieces)], axis=0))
    mixed = dot_nt(in_mix[0], high) + dot_nt(in_mix[0], low) + dot_nt(in_mix[1], high)
    out_s[...] = mixed.reshape(out_s.shape)
    stores[2].start()

    for k in range(2):
        @pl.when(send_ok[k])
        def _():
            row_copy(1, k).wait_send()
            row_copy(0, k).wait_send()
    for side in range(2):
        for dx in (0, -1, 1):
            ok = side_ok[side]
            if dx:
                ok = ok & (has_up if dx < 0 else has_down)

            @pl.when(ok)
            def _():
                strip_copy(side, dx).wait_send()
    wait_1.wait_send()
    wait_2.wait_send()
    if wait_3 is not None:
        wait_3.wait_send()
    for store in stores:
        store.wait()


def hand_on(prec, image, sketch, prec_out, image_out, sketch_out, held_p, held_i, held_s, load_sem, store_sem):
    loads, stores = [], []
    for part_no in range(HAND_ON_PARTS):
        for i, (source, held, target) in enumerate(
            ((sketch, held_s, sketch_out), (prec, held_p, prec_out), (image, held_i, image_out))
        ):
            size = held.shape[0] // HAND_ON_PARTS
            some = pl.ds(part_no * size, size)
            loads.append(pltpu.make_async_copy(source.at[some], held.at[some], load_sem.at[i, part_no]))
            stores.append(pltpu.make_async_copy(held.at[some], target.at[some], store_sem.at[i, part_no]))
    for load in loads:
        load.start()
    for load, store in zip(loads, stores):
        load.wait()
        store.start()
    for store in stores:
        store.wait()


def per_device(n_gx, n_gy, basis_vec, conductivity, sign_vals, sample_cols):
    depth, rows, cols = basis_vec.shape
    samples = sample_cols.shape[0]
    pieces = max(n_gy // COPIES, 1)
    share = samples // pieces
    wide, total = cols + 128, rows + 2 * HALO
    index = np.arange(rows)
    angle = (index[:, None] * index[None, :] % rows) * (2.0 * np.pi / rows)
    hartley = (np.cos(angle) + np.sin(angle)) / np.sqrt(rows)
    order = np.concatenate([np.arange(0, depth, 2), np.arange(1, depth, 2)])
    mix = np.einsum("jk,de->djke", hartley, np.eye(depth)[:, order]).reshape(depth * rows, rows * depth).astype(np.float32)
    mix_high = mix.astype(jnp.bfloat16)
    mix_low = (mix - mix_high.astype(np.float32)).astype(jnp.bfloat16)
    mix = jnp.asarray(np.stack([mix_high, mix_low]))

    field = (depth, rows, cols)
    tall = pltpu.VMEM((total, depth, wide), F32)
    scratch = [
        pltpu.VMEM(field, F32), pltpu.VMEM(field, F32), pltpu.VMEM((rows, cols), jnp.int32),
        pltpu.SMEM((samples,), jnp.int32), pltpu.VMEM(mix.shape, BF16),
        pltpu.VMEM((2, depth, HALO, cols), F32), pltpu.VMEM((2, depth, HALO, cols), F32),
        pltpu.VMEM((2, 2, depth, 128), F32), pltpu.VMEM((2, 3, 2, depth, 128), F32),
        tall, tall, tall, tall, tall, tall, tall, tall, tall,
        pltpu.VMEM((rows, depth, cols), F32), pltpu.VMEM((rows, depth, cols), F32),
        pltpu.VMEM((pieces, share, rows * depth), F32), pltpu.VMEM((n_gy, share, rows * depth), F32),
        pltpu.VMEM((share, rows * depth), F32), pltpu.VMEM((n_gx, share, rows * depth), F32),
        pltpu.VMEM((pieces, share, rows * depth), F32),
        pltpu.VMEM(field, F32), pltpu.VMEM(field, F32), pltpu.VMEM((depth, rows, samples), F32),
        pltpu.SemaphoreType.DMA((5,)), pltpu.SemaphoreType.DMA((3,)),
        pltpu.SemaphoreType.DMA((2, 2)), pltpu.SemaphoreType.DMA((2, 2)),
        pltpu.SemaphoreType.DMA((2, 3)), pltpu.SemaphoreType.DMA((2, 3)),
        pltpu.SemaphoreType.DMA((3,)), pltpu.SemaphoreType.DMA((3,)),
        pltpu.SemaphoreType.REGULAR((4,)), pltpu.SemaphoreType.REGULAR((4,)),
    ]
    results = pl.pallas_call(
        functools.partial(kernel, n_gx, n_gy),
        out_shape=(
            jax.ShapeDtypeStruct(field, F32),
            jax.ShapeDtypeStruct(field, F32),
            jax.ShapeDtypeStruct((depth, rows, samples), F32),
        ),
        in_specs=[pl.BlockSpec(memory_space=pl.ANY)] * 5,
        out_specs=(pl.BlockSpec(memory_space=pl.ANY),) * 3,
        scratch_shapes=scratch,
        compiler_params=pltpu.CompilerParams(
            collective_id=0, has_side_effects=True, vmem_limit_bytes=59000 * 1024
        ),
    )(basis_vec, conductivity, sign_vals, sample_cols, mix)
    return pl.pallas_call(
        hand_on,
        out_shape=tuple(jax.ShapeDtypeStruct(r.shape, F32) for r in results),
        in_specs=[pl.BlockSpec(memory_space=pl.ANY)] * 3,
        out_specs=(pl.BlockSpec(memory_space=pl.ANY),) * 3,
        scratch_shapes=[pltpu.VMEM(r.shape, F32) for r in results]
        + [pltpu.SemaphoreType.DMA((3, HAND_ON_PARTS)), pltpu.SemaphoreType.DMA((3, HAND_ON_PARTS))],
        compiler_params=pltpu.CompilerParams(vmem_limit_bytes=LAST_KIB * 1024),
    )(*results)


def solution(mesh):
    in_specs = (P(None, "gx", "gy"), P(None, "gx", "gy"), P("gx", "gy"), P("gy"))
    out_specs = (P(None, "gx", "gy"), P(None, "gx", "gy"), P(None, "gx", None))
    return jax.shard_map(
        functools.partial(per_device, mesh.shape["gx"], mesh.shape["gy"]),
        mesh=mesh, in_specs=in_specs, out_specs=out_specs, check_vma=False,
    )
```
